32 devices in a mesh: lat: 4 (over y, x), lon: 8 (over z, core).
Axes of the slice: x: 2, y: 2, z: 4, core: 2. Of those that a mesh axis runs over, the one named last changes fastest.
Arguments:
- target: float32 [3, 256, 4096], P(None, 'lat', 'lon'), may hold values from -8 to 8
- latent_0: float32 [256, 4096], P('lat', 'lon'), may hold values from -10 to 10
- latent_1: float32 [128, 2048], P('lat', 'lon'), may hold values from -10 to 10
- latent_2: float32 [64, 1024], P('lat', 'lon'), may hold values from -10 to 10
- latent_3: float32 [32, 512], P('lat', 'lon'), may hold values from -10 to 10
- latent_4: float32 [16, 256], P('lat', 'lon'), may hold values from -10 to 10
- latent_5: float32 [8, 128], P('lat', 'lon'), may hold values from -10 to 10
- tile_seeds: int32 [4, 8], P('lat', 'lon'), may hold values from 0 to 1073741823
- anchor_parity: int32 [6], replicated, may hold values from 0 to 1
- anchor_scale: float32 [6], replicated, may hold values from 0.5 to 4
- mix_levels: bfloat16 [24, 6], replicated, may hold values from -2.5 to 2.5
- mix_hidden: bfloat16 [24, 24], replicated, may hold values from -1.25 to 1.25
- conv_first: bfloat16 [24, 24, 3, 3], replicated, may hold values from -0.4375 to 0.4375
- conv_second: bfloat16 [24, 24, 3, 3], replicated, may hold values from -0.4375 to 0.4375
- conv_output: bfloat16 [3, 24, 3, 3], replicated, may hold values from -0.4375 to 0.4375
- context_in: float32 [24, 12], replicated, may hold values from -1.75 to 1.75
- context_mid: float32 [24, 24], replicated, may hold values from -1.25 to 1.25
- context_out: float32 [2, 24], replicated, may hold values from -1.25 to 1.25
Outputs:
- reconstruction: float32 [3, 256, 4096], P(None, 'lat', 'lon')
- bits_finest: float32 [256, 4096], P('lat', 'lon')
- loss_terms: float32 [7], replicated
- output_grad: float32 [3, 24, 3, 3], replicated
The draws below stay inside these ranges and needn't reach their ends.
All inputs are finite; a program needn't handle non-finite values.
Results may differ from the reference program's by a relative error of at most 0.00035.
The reference program's roundings to bfloat16 on the way (of `upsampled`, `first`, `second`, `third`, `fourth` and `slope`) count: a program that leaves them out, or rounds other values in their place, can miss the bound.
Values may be sent and summed in bfloat16 or wider, within the bound.
A program may use at most 128 MiB of HBM per device.

```python
import math
import jax
import jax.numpy as jnp
from jax import lax

H_DEV = 64
W_DEV = 512
LEVELS = 6
CH = 24
ARM_WIDTH = 24
CTX = 12
BANDS = 3
NH = 256
NW = 4096
TILE_ROWS = 4
TILE_COLS = 8


def draw_target(key, part):
    first_key, second_key = jax.random.split(jax.random.fold_in(key, 11))
    rows_pos = jnp.arange(NH, dtype=jnp.float32) / NH
    cols_pos = jnp.arange(NW, dtype=jnp.float32) / NW
    trend = 0.4 * jnp.power(3.0, cols_pos)[None, None, :] * jnp.power(2.0, rows_pos)[None, :, None]
    rough = jax.random.uniform(second_key, (BANDS, NH, NW), jnp.float32, 0.5, 1.5)
    values = jax.random.normal(first_key, (BANDS, NH, NW), jnp.float32) * rough * trend
    return jnp.clip(values, -8.0, 8.0)


def with_ends(values, key, least, high):
    extent = values.shape
    place = [jax.random.randint(jax.random.fold_in(key, axis), (), 0, extent[axis]) for axis in range(len(extent))]
    values = values.at[tuple(place)].set(least)
    longest = extent.index(max(extent))
    place[longest] = (place[longest] + 1) % extent[longest]
    return values.at[tuple(place)].set(high)


def shard_levels(rng, dims, pieces, smallest, top_value):
    def one(dim, blocks):
        heights = jax.random.uniform(jax.random.fold_in(jax.random.fold_in(rng, 6), dim), (blocks,), jnp.float32, smallest / len(pieces), top_value / len(pieces))
        return jnp.repeat(jnp.exp(heights), dims[dim] // blocks).reshape((-1,) + (1,) * (len(dims) - dim - 1))

    level = one(*pieces[0])
    for cut in pieces[1:]:
        level = level * one(*cut)
    return level


def gaussian(own_key, shape, scale, reach, pieces=(), kind=jnp.bfloat16):
    level = shard_levels(own_key, shape, pieces, -0.22, 0.18) if pieces else 1.0
    values = jax.random.normal(own_key, shape, jnp.float32) * scale * level
    return jnp.minimum(jnp.maximum(values, -reach), reach).astype(kind)


def setup_inputs(seed: int = 0) -> dict:
    key_of = jax.random.split(jax.random.key(seed), 19)
    target = draw_target(jax.random.fold_in(key_of[18], 71), 0)
    latent_0 = gaussian(key_of[1], (NH, NW), 2.0, 10.0, ((0, 4), (1, 8)), jnp.float32)
    latent_1 = gaussian(key_of[2], (NH // 2, NW // 2), 2.0, 10.0, ((0, 4), (1, 8)), jnp.float32)
    latent_2 = gaussian(key_of[3], (NH // 4, NW // 4), 2.0, 10.0, ((0, 4), (1, 8)), jnp.float32)
    latent_3 = gaussian(key_of[4], (NH // 8, NW // 8), 2.0, 10.0, ((0, 4), (1, 8)), jnp.float32)
    latent_4 = gaussian(key_of[5], (NH // 16, NW // 16), 2.0, 10.0, ((0, 4), (1, 8)), jnp.float32)
    latent_5 = gaussian(key_of[6], (NH // 32, NW // 32), 2.0, 10.0, ((0, 4), (1, 8)), jnp.float32)
    tile_seeds = with_ends(jax.random.randint(key_of[7], (TILE_ROWS, TILE_COLS), 0, 1073741824), jax.random.fold_in(key_of[7], 1), 0, 1073741823).astype(jnp.int32)
    anchor_parity = with_ends(jax.random.randint(key_of[8], (LEVELS,), 0, 2), jax.random.fold_in(key_of[8], 1), 0, 1).astype(jnp.int32)
    anchor_scale = jnp.clip(jnp.exp(jax.random.uniform(key_of[9], (LEVELS,), jnp.float32, math.log(0.5), math.log(4.0))), 0.5, 4.0)
    mix_levels = gaussian(key_of[10], (CH, LEVELS), LEVELS ** -0.5, 2.5)
    mix_hidden = gaussian(key_of[11], (CH, CH), CH ** -0.5, 1.25)
    conv_first = gaussian(key_of[12], (CH, CH, 3, 3), (9 * CH) ** -0.5, 0.4375)
    conv_second = gaussian(key_of[13], (CH, CH, 3, 3), (9 * CH) ** -0.5, 0.4375)
    conv_output = gaussian(key_of[14], (BANDS, CH, 3, 3), (9 * CH) ** -0.5, 0.4375)
    context_in = gaussian(key_of[15], (ARM_WIDTH, CTX), CTX ** -0.5, 1.75, (), jnp.float32)
    context_mid = gaussian(key_of[16], (ARM_WIDTH, ARM_WIDTH), ARM_WIDTH ** -0.5, 1.25, (), jnp.float32)
    context_out = gaussian(key_of[17], (2, ARM_WIDTH), ARM_WIDTH ** -0.5, 1.25, (), jnp.float32)
    return {"target": target, "latent_0": latent_0, "latent_1": latent_1, "latent_2": latent_2, "latent_3": latent_3, "latent_4": latent_4, "latent_5": latent_5, "tile_seeds": tile_seeds, "anchor_parity": anchor_parity, "anchor_scale": anchor_scale, "mix_levels": mix_levels, "mix_hidden": mix_hidden, "conv_first": conv_first, "conv_second": conv_second, "conv_output": conv_output, "context_in": context_in, "context_mid": context_mid, "context_out": context_out}


mix_level = 668265263
mix_row = 374761393
mix_col = 1103515245
mix_mult = 73244475
log_two = 0.6931471805599453
context_steps = ((-1, 0), (1, 0), (0, -1), (0, 1), (-2, -1), (-2, 1), (2, -1), (2, 1), (-1, -2), (-1, 2), (1, -2), (1, 2))


def logical_shift(value, places):
    return jnp.bitwise_and(jnp.right_shift(value, jnp.int32(places)), jnp.int32((1 << (32 - places)) - 1))


def hashed_noise(seed_value, level_index, local_rows, local_cols):
    value = seed_value + jnp.int32(level_index) * jnp.int32(mix_level)
    value = value + local_rows[:, None] * jnp.int32(mix_row) + local_cols[None, :] * jnp.int32(mix_col)
    value = jnp.bitwise_xor(value, logical_shift(value, 15))
    value = value * jnp.int32(mix_mult)
    value = jnp.bitwise_xor(value, logical_shift(value, 13))
    value = value * jnp.int32(mix_mult)
    value = jnp.bitwise_xor(value, logical_shift(value, 16))
    return jnp.bitwise_and(value, jnp.int32(16777215)).astype(jnp.float32) / 16777216.0 - 0.5


def upsample_axis(extended, factor, along):
    cells_in = extended.shape[along] - 2
    earlier = lax.slice_in_dim(extended, 0, cells_in, axis=along)
    current = lax.slice_in_dim(extended, 1, cells_in + 1, axis=along)
    following = lax.slice_in_dim(extended, 2, cells_in + 2, axis=along)
    position = (jnp.arange(factor, dtype=jnp.float32) + 0.5) / factor - 0.5
    weight_low = jnp.maximum(-position, 0.0)
    weight_high = jnp.maximum(position, 0.0)
    weight_mid = 1.0 - weight_low - weight_high
    view_shape = [1] * (extended.ndim + 1)
    view_shape[along + 1] = factor
    result = jnp.expand_dims(earlier, along + 1) * weight_low.reshape(view_shape)
    result = result + jnp.expand_dims(current, along + 1) * weight_mid.reshape(view_shape)
    result = result + jnp.expand_dims(following, along + 1) * weight_high.reshape(view_shape)
    new_shape = list(extended.shape)
    new_shape[along] = cells_in * factor
    return result.reshape(new_shape)


def laplace_bits(offset, spread):
    magnitude = jnp.abs(offset)
    outer = jnp.log(0.5) - (jnp.maximum(magnitude, 0.5) - 0.5) / spread + jnp.log(-jnp.expm1(-1.0 / spread))
    inner_offset = jnp.clip(offset, -0.5, 0.5)
    inner = jnp.log(1.0 - 0.5 * (jnp.exp(-(0.5 - inner_offset) / spread) + jnp.exp(-(0.5 + inner_offset) / spread)))
    return -jnp.where(magnitude >= 0.5, outer, inner) / log_two


def level_bits(extended, context_in, context_mid, context_out, anchor_value, parity_bit, row_start, col_start):
    rows_in = extended.shape[0] - 4
    cols_in = extended.shape[1] - 4
    context = jnp.stack([extended[2 + row_step:2 + row_step + rows_in, 2 + col_step:2 + col_step + cols_in] for row_step, col_step in context_steps])
    quantized = extended[2:2 + rows_in, 2:2 + cols_in]
    highest = lax.Precision.HIGHEST
    inner = jax.nn.relu(jnp.einsum("hk,kyx->hyx", context_in, context, precision=highest))
    outer = jax.nn.relu(jnp.einsum("hg,gyx->hyx", context_mid, inner, precision=highest))
    raw_out = jnp.einsum("oh,hyx->oyx", context_out, outer, precision=highest)
    row_ids = row_start + jnp.arange(rows_in, dtype=jnp.int32)
    col_ids = col_start + jnp.arange(cols_in, dtype=jnp.int32)
    anchor = ((row_ids[:, None] + col_ids[None, :] + parity_bit) % 2) == 0
    centre = jnp.where(anchor, 0.0, raw_out[0])
    spread = jnp.where(anchor, anchor_value, 0.1 + jax.nn.softplus(raw_out[1]))
    return laplace_bits(quantized - centre, spread)


def conv_rows(field, kernel, row_pad):
    return lax.conv_general_dilated(field[None], kernel, (1, 1), ((row_pad, row_pad), (0, 0)), dimension_numbers=("NCHW", "OIHW", "NCHW"), preferred_element_type=jnp.float32)[0]


def reference(target, latent_0, latent_1, latent_2, latent_3, latent_4, latent_5, tile_seeds, anchor_parity, anchor_scale, mix_levels, mix_hidden, conv_first, conv_second, conv_output, context_in, context_mid, context_out):
    latents = (latent_0, latent_1, latent_2, latent_3, latent_4, latent_5)
    quantized_levels = []
    for level_index in range(LEVELS):
        tile_rows = H_DEV // 2 ** level_index
        tile_cols = W_DEV // 2 ** level_index
        row_ids = jnp.arange(NH // 2 ** level_index, dtype=jnp.int32)
        col_ids = jnp.arange(NW // 2 ** level_index, dtype=jnp.int32)
        seed_field = tile_seeds[(row_ids // tile_rows)[:, None], (col_ids // tile_cols)[None, :]]
        noise = hashed_noise(seed_field, level_index, row_ids % tile_rows, col_ids % tile_cols)
        quantized_levels.append(latents[level_index] + noise)
    pixel_count = BANDS * NH * NW

    def one_block(block_index):
        col_start = block_index * W_DEV
        up_layers = []
        bit_sums = []
        bits_top = None
        for level_index in range(LEVELS):
            factor = 2 ** level_index
            cols_level = W_DEV // factor
            total_cols = NW // factor
            spare = (3 + factor - 1) // factor
            column_ids = (block_index * cols_level + jnp.arange(-spare - 1, cols_level + spare + 1, dtype=jnp.int32)) % total_cols
            rowed = jnp.pad(jnp.take(quantized_levels[level_index], column_ids, axis=1), ((1, 1), (0, 0)))
            grown = upsample_axis(upsample_axis(rowed, factor, 0), factor, 1)
            margin = spare * factor - 3
            up_layers.append(grown[:, margin:margin + W_DEV + 6])
            near_ids = (block_index * cols_level + jnp.arange(-2, cols_level + 2, dtype=jnp.int32)) % total_cols
            extended = jnp.pad(jnp.take(quantized_levels[level_index], near_ids, axis=1), ((2, 2), (0, 0)))
            bits = level_bits(extended, context_in, context_mid, context_out, anchor_scale[level_index], anchor_parity[level_index], jnp.int32(0), block_index * cols_level)
            if level_index == 0:
                bits_top = bits
            bit_sums.append(jnp.sum(bits))
        upsampled = jnp.stack(up_layers).astype(jnp.bfloat16)
        first = jax.nn.relu(jnp.einsum("cl,lhw->chw", mix_levels, upsampled, preferred_element_type=jnp.float32)).astype(jnp.bfloat16)
        second = jax.nn.relu(jnp.einsum("cd,dhw->chw", mix_hidden, first, preferred_element_type=jnp.float32)).astype(jnp.bfloat16)
        third = (second[:, :, 1:-1] + jax.nn.relu(conv_rows(second, conv_first, 1))).astype(jnp.bfloat16)
        fourth = (third[:, :, 1:-1] + jax.nn.relu(conv_rows(third, conv_second, 1))).astype(jnp.bfloat16)
        padded = jnp.pad(fourth, ((0, 0), (1, 1), (0, 0)))
        recon = conv_rows(padded, conv_output, 0)
        error = recon - lax.dynamic_slice_in_dim(target, col_start, W_DEV, 2)
        squared = jnp.sum(error * error)
        slope = (2.0 * error / pixel_count).astype(jnp.bfloat16)
        taps = []
        for row_tap in range(3):
            for col_tap in range(3):
                window = padded[:, row_tap:row_tap + NH, col_tap:col_tap + W_DEV]
                taps.append(jnp.einsum("ohw,chw->oc", slope, window, preferred_element_type=jnp.float32))
        gradient = jnp.stack(taps, axis=-1).reshape(BANDS, slope.shape[0] * 0 + fourth.shape[0], 3, 3)
        return recon, bits_top, jnp.stack(bit_sums), squared, gradient

    recons, tops, level_sums, squares, gradients = lax.map(one_block, jnp.arange(NW // W_DEV, dtype=jnp.int32))
    reconstruction = recons.transpose(1, 2, 0, 3).reshape(BANDS, NH, NW)
    bits_finest = tops.transpose(1, 0, 2).reshape(NH, NW)
    cells = jnp.array([(NH // 2 ** level_index) * (NW // 2 ** level_index) for level_index in range(LEVELS)], dtype=jnp.float32)
    loss_terms = jnp.concatenate([jnp.sum(squares)[None] / pixel_count, jnp.sum(level_sums, axis=0) / cells])
    return reconstruction, bits_finest, loss_terms, jnp.sum(gradients, axis=0)
```

```python
import functools

import jax
import jax.numpy as jnp
from jax import lax
from jax.experimental import pallas as pl
from jax.experimental.pallas import tpu as pltpu
from jax.sharding import PartitionSpec as P

mix_level = 668265263
mix_row = 374761393
mix_col = 1103515245
mix_mult = 73244475
log_two = 0.6931471805599453
context_steps = (
    (-1, 0),
    (1, 0),
    (0, -1),
    (0, 1),
    (-2, -1),
    (-2, 1),
    (2, -1),
    (2, 1),
    (-1, -2),
    (-1, 2),
    (1, -2),
    (1, 2),
)
MESH = pl.DeviceIdType.MESH
BF = jnp.bfloat16
F32 = jnp.float32
LANES = 128
SUB = 8


def width_of(cols):
    return cols + LANES if cols >= LANES else LANES


def iota(shape, dim):
    return lax.broadcasted_iota(jnp.int32, shape, dim)


def hashed_noise(seed_value, level_index, shape):
    value = seed_value + jnp.int32(level_index * mix_level % (1 << 32) - (1 << 32) * ((level_index * mix_level % (1 << 32)) >> 31))
    value = value + iota(shape, 0) * jnp.int32(mix_row) + iota(shape, 1) * jnp.int32(mix_col)
    value = value ^ lax.shift_right_logical(value, jnp.full(shape, 15, jnp.int32))
    value = value * jnp.int32(mix_mult)
    value = value ^ lax.shift_right_logical(value, jnp.full(shape, 13, jnp.int32))
    value = value * jnp.int32(mix_mult)
    value = value ^ lax.shift_right_logical(value, jnp.full(shape, 16, jnp.int32))
    return (value & jnp.int32(16777215)).astype(F32) / 16777216.0 - 0.5


def halo_kernel(shapes, seed_ref, *refs):
    n = len(shapes)
    latents, ext = refs[:n], refs[n : 2 * n]
    send_l, send_r, recv_r, recv_l, send_u, send_d, recv_b, recv_t, ssem, rsem = refs[2 * n :]
    lat, lon = lax.axis_index("lat"), lax.axis_index("lon")
    lats, lons = lax.axis_size("lat"), lax.axis_size("lon")
    left, right = (lat, lax.rem(lon + lons - 1, lons)), (lat, lax.rem(lon + 1, lons))
    up, down = (lax.rem(lat + lats - 1, lats), lon), (lax.rem(lat + 1, lats), lon)
    barrier = pltpu.get_barrier_semaphore()
    for other in (left, right, up, down):
        pl.semaphore_signal(barrier, inc=1, device_id=other, device_id_type=MESH)
    seed = seed_ref[0, 0]
    row = 0
    for level, (rows, cols) in enumerate(shapes):
        e = ext[level]
        tall = max(rows, SUB)
        e[...] = jnp.zeros_like(e)
        e[SUB : SUB + rows, 0:cols] = latents[level][...] + hashed_noise(seed, level, (rows, cols))
        if cols >= LANES:
            send_l[row : row + tall, :] = e[SUB : SUB + tall, 0:LANES]
            send_r[row : row + tall, :] = e[SUB : SUB + tall, cols - LANES : cols]
        else:
            whole = e[SUB : SUB + tall, :]
            send_l[row : row + tall, :] = whole
            send_r[row : row + tall, :] = pltpu.roll(whole, LANES - cols, 1)
        row += tall
    pl.semaphore_wait(barrier, 4)

    def copy(src, dst, index, other):
        return pltpu.make_async_remote_copy(
            src_ref=src,
            dst_ref=dst,
            send_sem=ssem.at[index],
            recv_sem=rsem.at[index],
            device_id=other,
            device_id_type=MESH,
        )

    to_left = copy(send_l, recv_r, 0, left)
    to_right = copy(send_r, recv_l, 1, right)
    to_left.start()
    to_right.start()
    to_left.wait()
    to_right.wait()
    row = 0
    lane0 = 0
    for level, (rows, cols) in enumerate(shapes):
        e = ext[level]
        tall = max(rows, SUB)
        from_right = recv_r[row : row + tall, :]
        from_left = recv_l[row : row + tall, :]
        lane = iota((tall, LANES), 1)
        if cols >= LANES:
            e[SUB : SUB + tall, cols : cols + LANES] = jnp.where(
                lane < LANES // 2, from_right, from_left
            )
        else:
            whole = e[SUB : SUB + tall, :]
            moved = pltpu.roll(from_right, cols, 1)
            halo = jnp.where(
                lane < cols + 4, moved, jnp.where(lane >= LANES - 4, from_left, 0.0)
            )
            e[SUB : SUB + tall, :] = jnp.where(lane < cols, whole, halo)
        wide = width_of(cols)
        send_u[:, lane0 : lane0 + wide] = e[SUB : 2 * SUB, :]
        send_d[:, lane0 : lane0 + wide] = e[tall : tall + SUB, :]
        row += tall
        lane0 += wide
    to_up = copy(send_u, recv_b, 2, up)
    to_down = copy(send_d, recv_t, 3, down)
    to_up.start()
    to_down.start()
    to_up.wait()
    to_down.wait()
    keep_t = jnp.where(lat > 0, 1.0, 0.0).astype(F32)
    keep_b = jnp.where(lat < lats - 1, 1.0, 0.0).astype(F32)
    lane0 = 0
    for level, (rows, cols) in enumerate(shapes):
        e = ext[level]
        wide = width_of(cols)
        top = recv_t[:, lane0 : lane0 + wide] * keep_t
        bottom = recv_b[:, lane0 : lane0 + wide] * keep_b
        reach = min(rows, SUB)
        e[SUB - reach : SUB, :] = top[:reach]
        e[SUB + rows : SUB + rows + reach, :] = bottom[:reach]
        lane0 += wide


def dot(a, b):
    return jnp.dot(a, b, preferred_element_type=F32)


def parts(x, count):
    out = []
    for _ in range(count):
        piece = x.astype(BF)
        out.append(piece)
        x = x - piece.astype(F32)
    return out


def dot_pairs(a, x):
    hi, lo = parts(x, 2)
    return dot(a[0], hi) + (dot(a[1], hi) + dot(a[0], lo))


def div_24(x):
    return (x * 2731) >> 16


def one_hot(flag):
    return jnp.where(flag, 1.0, 0.0).astype(BF)


def laplace_bits(offset, spread):
    magnitude = jnp.abs(offset)
    t = 1.0 / spread
    series = t * (1.0 - t * (0.5 - t * (1.0 / 6 - t * (1.0 / 24 - t * (1.0 / 120)))))
    gap = jnp.where(t < 0.1, series, 1.0 - jnp.exp(-t))
    outer = -log_two - (jnp.maximum(magnitude, 0.5) - 0.5) / spread + jnp.log(gap)
    inner_offset = jnp.clip(offset, -0.5, 0.5)
    inner = jnp.log(
        1.0
        - 0.5 * (jnp.exp(-(0.5 - inner_offset) / spread) + jnp.exp(-(0.5 + inner_offset) / spread))
    )
    return jnp.where(magnitude >= 0.5, outer, inner) * (-1.0 / log_two)


def local_kernel(shapes, ch, bands, pixel_count, *refs):
    n = len(shapes)
    ext = refs[:n]
    (
        target, parity, anchor, mix_l, mix_h, taps, c_in, c_mid, c_out,
        recon, bits_out, part, ups, second, third, fourth,
    ) = refs[n:]
    lat, lon = lax.axis_index("lat"), lax.axis_index("lon")
    lats = lax.axis_size("lat")
    rows_dev, cols_dev = shapes[0]
    wide = width_of(cols_dev)
    deep = SUB * ch
    reach = (SUB + 2) * ch
    stride = taps.shape[0] // 9

    lane_ch = iota((ch, deep), 1)
    fold = one_hot(lane_ch - ch * div_24(lane_ch) == iota((ch, deep), 0))
    same_row = div_24(iota((deep, deep), 0)) == div_24(iota((deep, deep), 1))

    def block_diagonal(w):
        return jnp.where(same_row, jnp.concatenate([dot(w, fold)] * SUB, 0), 0.0).astype(BF)

    def row_inside(w):
        k = w.shape[1]
        spread = one_hot((iota((k, k * SUB), 1) >> 3) == iota((k, k * SUB), 0))
        shape = (deep, k * SUB)
        keep = (iota(shape, 1) & 7) == div_24(iota(shape, 0))
        return jnp.where(keep, jnp.concatenate([dot(w, spread)] * SUB, 0), 0.0).astype(BF)

    def rows_out(w):
        wide_w = dot(w, fold)
        grown = jnp.concatenate(
            [jnp.broadcast_to(wide_w[o : o + 1], (SUB, deep)) for o in range(w.shape[0])], 0
        )
        shape = (w.shape[0] * SUB, deep)
        keep = (iota(shape, 0) & 7) == div_24(iota(shape, 1))
        return jnp.where(keep, grown, 0.0).astype(BF)

    t_levels = row_inside(mix_l[...])
    t_hidden = block_diagonal(mix_h[...])
    a_in = [row_inside(p) for p in parts(c_in[...], 2)]
    a_mid = [block_diagonal(p) for p in parts(c_mid[...], 2)]
    a_out = [rows_out(p) for p in parts(c_out[...], 2)]

    lane_re = iota((ch, reach), 1)
    fold_re = one_hot(lane_re - ch * div_24(lane_re) == iota((ch, reach), 0))
    wide_taps = dot(taps[...], fold_re)
    step = div_24(iota((deep, reach), 1)) - div_24(iota((deep, reach), 0))
    step_out = div_24(iota((bands * SUB, reach), 1)) - (iota((bands * SUB, reach), 0) & 7)

    def conv_taps(first_row):
        out = []
        for b in range(3):
            total = jnp.zeros((deep, reach), F32)
            for a in range(3):
                at = (3 * a + b) * stride + first_row
                total = jnp.where(
                    step == a, jnp.concatenate([wide_taps[at : at + ch]] * SUB, 0), total
                )
            out.append(total.astype(BF))
        return jnp.concatenate(out, 0)

    def output_taps():
        out = []
        for b in range(3):
            total = jnp.zeros((bands * SUB, reach), F32)
            for a in range(3):
                at = (3 * a + b) * stride + 2 * ch
                grown = jnp.concatenate(
                    [
                        jnp.broadcast_to(wide_taps[at + o : at + o + 1], (SUB, reach))
                        for o in range(bands)
                    ],
                    0,
                )
                total = jnp.where(step_out == a, grown, total)
            out.append(total)
        return jnp.concatenate(out, 0).astype(BF)

    t_first = conv_taps(0)
    t_second = conv_taps(ch)
    t_output = output_taps()

    tall_up = ups.shape[1]
    ups[0] = ext[0][SUB - 3 : SUB - 3 + tall_up, :]
    for level in range(1, n):
        rows, cols = shapes[level]
        e = ext[level]
        scale = 2.0 ** -level
        shape = (tall_up, e.shape[0])
        where_to = ((iota(shape, 0) - 3).astype(F32) + 0.5) * scale - 0.5
        along = jnp.maximum(
            0.0, 1.0 - jnp.abs(where_to - (iota(shape, 1) - SUB).astype(F32))
        ).astype(BF)
        hi, mid, lo = [dot(along, p) for p in parts(e[...], 3)]
        grown = hi + (mid + lo)
        shape = (e.shape[1], wide)
        pixel = iota(shape, 1)
        pixel = jnp.where(pixel < cols_dev + LANES // 2, pixel, pixel - wide)
        cell = iota(shape, 0)
        cell = jnp.where(cell < (cols + e.shape[1]) // 2, cell, cell - e.shape[1])
        where_to = (pixel.astype(F32) + 0.5) * scale - 0.5
        along = jnp.maximum(0.0, 1.0 - jnp.abs(where_to - cell.astype(F32))).astype(BF)
        hi, mid, lo = [dot(p, along) for p in parts(grown, 3)]
        ups[level] = hi + (mid + lo)

    def inside(field, start, margin):
        index = iota(field.shape, 0)
        begin = margin - start - lat * rows_dev
        keep = (index >= begin * ch) & (index < (begin + rows_dev * lats) * ch)
        return jnp.where(keep, field, 0.0)

    def mix_step(g, carry):
        here = pl.ds(pl.multiple_of(g * SUB, SUB), SUB)
        x = jnp.concatenate([ups[level, here, :] for level in range(n)], 0).astype(BF)
        f = jnp.maximum(dot(t_levels, x), 0.0).astype(BF)
        s = jnp.maximum(dot(t_hidden, f), 0.0)
        second[pl.ds(pl.multiple_of(g * deep, deep), deep), :] = inside(s, g * SUB, 3).astype(BF)
        return carry

    lax.fori_loop(0, tall_up // SUB, mix_step, 0)

    def conv_pass(src, dst, weights, count, margin):
        def step_fn(k, carry):
            start = jnp.minimum(k * SUB, count - SUB)
            at = pl.multiple_of(start * ch, 2 * ch)
            x = src[pl.ds(at, reach), :]
            p = dot(weights, x)
            c = (
                p[deep : 2 * deep]
                + pltpu.roll(p[:deep], 1, 1)
                + pltpu.roll(p[2 * deep :], wide - 1, 1)
            )
            r = x.astype(F32)[ch : ch + deep] + jnp.maximum(c, 0.0)
            dst[pl.ds(at, deep), :] = inside(r, start, margin).astype(BF)
            return carry

        lax.fori_loop(0, (count + SUB - 1) // SUB, step_fn, 0)

    conv_pass(second, third, t_first, rows_dev + 4, 2)
    conv_pass(third, fourth, t_second, rows_dev + 2, 1)

    def output_step(k, carry):
        squares, grad = carry
        x = fourth[pl.ds(pl.multiple_of(k * deep, deep), reach), :]
        p = dot(t_output, x)
        m = bands * SUB
        c = p[m : 2 * m] + pltpu.roll(p[:m], 1, 1) + pltpu.roll(p[2 * m :], wide - 1, 1)
        c = c[:, :cols_dev]
        here = pl.ds(pl.multiple_of(k * SUB, SUB), SUB)
        for o in range(bands):
            recon[o, here, :] = c[o * SUB : (o + 1) * SUB]
        error = c - jnp.concatenate([target[o, here, :] for o in range(bands)], 0)
        slope = (2.0 * error / pixel_count).astype(BF).astype(F32)
        slope = jnp.concatenate([slope, jnp.zeros((m, wide - cols_dev), F32)], 1)
        slopes = jnp.concatenate(
            [pltpu.roll(slope, wide - 1, 1), slope, pltpu.roll(slope, 1, 1)], 0
        ).astype(BF)
        grad = grad + lax.dot_general(
            slopes, x, (((1,), (1,)), ((), ())), preferred_element_type=F32
        )
        return squares + error * error, grad

    m = bands * SUB
    squares, grad = lax.fori_loop(
        0,
        rows_dev // SUB,
        output_step,
        (jnp.zeros((m, cols_dev), F32), jnp.zeros((3 * m, reach), F32)),
    )
    pad = -reach % LANES
    grad = jnp.concatenate([grad, jnp.zeros((3 * m, pad), F32)], 1)
    line = iota(grad.shape, 0) & 7
    aligned = grad
    for y in range(1, SUB):
        aligned = jnp.where(line == y, pltpu.roll(grad, reach + pad - y * ch, 1), aligned)
    folded = jnp.sum(aligned[:, :LANES].reshape(3 * bands, SUB, LANES), axis=1)
    sums = jnp.concatenate([folded, jnp.zeros((part.shape[0] - 3 * bands, LANES), F32)], 0)

    shape = part.shape
    last = iota(shape, 0) == 3 * bands

    def put(sums, lane, value):
        return jnp.where(last & (iota(shape, 1) == lane), value, sums)

    sums = put(sums, 0, jnp.sum(squares))

    for level, (rows, cols) in enumerate(shapes):
        e = ext[level]
        cover = max(cols, LANES)
        full = e.shape[1]
        scale = anchor[level]
        odd = lat * rows + lon * cols + parity[level]

        def rate_step(g, total, level=level, rows=rows, cols=cols, e=e, cover=cover, full=full, scale=scale, odd=odd):
            window = e[pl.ds(pl.multiple_of(g * SUB, SUB), 3 * SUB), :]
            moved = {i: window[SUB + i : 2 * SUB + i] for i in range(-2, 3)}
            context = [
                (moved[i] if j == 0 else pltpu.roll(moved[i], (-j) % full, 1))[:, :cover]
                for i, j in context_steps
            ]
            inner = jnp.maximum(dot_pairs(a_in, jnp.concatenate(context, 0)), 0.0)
            outer = jnp.maximum(dot_pairs(a_mid, inner), 0.0)
            raw = dot_pairs(a_out, outer)
            mu, sigma = raw[:SUB], raw[SUB:]
            row, col = iota((SUB, cover), 0), iota((SUB, cover), 1)
            first = ((row + col + odd) & 1) == 0
            centre = jnp.where(first, 0.0, mu)
            soft = jnp.maximum(sigma, 0.0) + jnp.log1p(jnp.exp(-jnp.abs(sigma)))
            spread = jnp.where(first, scale, 0.1 + soft)
            bits = laplace_bits(moved[0][:, :cover] - centre, spread)
            if level == 0:
                bits_out[pl.ds(pl.multiple_of(g * SUB, SUB), SUB), :] = bits
            if rows < SUB or cols < LANES:
                bits = jnp.where((row < rows) & (col < cols), bits, 0.0)
            return total + bits

        total = lax.fori_loop(0, max(1, rows // SUB), rate_step, jnp.zeros((SUB, cover), F32))
        sums = put(sums, 1 + level, jnp.sum(total))
    part[...] = sums


def local(target, *args):
    latents = args[:-11]
    (
        tile_seeds, anchor_parity, anchor_scale, mix_levels, mix_hidden,
        conv_first, conv_second, conv_output, context_in, context_mid, context_out,
    ) = args[-11:]
    n = len(latents)
    shapes = [x.shape for x in latents]
    bands, rows_dev, cols_dev = target.shape
    ch = mix_hidden.shape[0]
    devices = lax.axis_size("lat") * lax.axis_size("lon")
    pixel_count = float(bands * rows_dev * cols_dev * devices)
    vmem = pl.BlockSpec(memory_space=pltpu.VMEM)
    smem = pl.BlockSpec(memory_space=pltpu.SMEM)
    wides = [width_of(c) for _, c in shapes]
    talls = [max(r, SUB) for r, _ in shapes]
    edge = pltpu.VMEM((sum(talls), LANES), F32)
    belt = pltpu.VMEM((SUB, sum(wides)), F32)
    extended = pl.pallas_call(
        functools.partial(halo_kernel, shapes),
        out_shape=[
            jax.ShapeDtypeStruct((t + 2 * SUB, w), F32) for t, w in zip(talls, wides)
        ],
        in_specs=[smem] + [vmem] * n,
        out_specs=[vmem] * n,
        scratch_shapes=[edge] * 4
        + [belt] * 4
        + [pltpu.SemaphoreType.DMA((4,)), pltpu.SemaphoreType.DMA((4,))],
        compiler_params=pltpu.CompilerParams(
            collective_id=0, has_side_effects=True, vmem_limit_bytes=16 * 2**20
        ),
        name="halo",
    )(tile_seeds, *latents)
    taps = jnp.concatenate([conv_first, conv_second, conv_output], 0).transpose(2, 3, 0, 1)
    taps = jnp.pad(taps, ((0, 0), (0, 0), (0, -taps.shape[2] % SUB), (0, 0))).reshape(-1, ch)
    wide = wides[0]
    tall_up = rows_dev + SUB
    recon, bits, part = pl.pallas_call(
        functools.partial(local_kernel, shapes, ch, bands, pixel_count),
        out_shape=[
            jax.ShapeDtypeStruct(target.shape, F32),
            jax.ShapeDtypeStruct((rows_dev, cols_dev), F32),
            jax.ShapeDtypeStruct((2 * SUB, LANES), F32),
        ],
        in_specs=[vmem] * (n + 1) + [smem] * 2 + [vmem] * 6,
        out_specs=[vmem] * 3,
        scratch_shapes=[
            pltpu.VMEM((n, tall_up, wide), F32),
            pltpu.VMEM((tall_up * ch, wide), BF),
            pltpu.VMEM(((rows_dev + 4) * ch, wide), BF),
            pltpu.VMEM(((rows_dev + 2) * ch, wide), BF),
        ],
        compiler_params=pltpu.CompilerParams(vmem_limit_bytes=48 * 2**20),
        name="step",
    )(
        *extended, target, anchor_parity, anchor_scale, mix_levels, mix_hidden,
        taps, context_in, context_mid, context_out,
    )
    total = lax.psum(part, ("lat", "lon"))
    grad = total[: 3 * bands, : 3 * ch].reshape(3, bands, 3, ch).transpose(1, 3, 2, 0)
    counts = jnp.array(
        [pixel_count] + [float(r * c * devices) for r, c in shapes], dtype=F32
    )
    loss_terms = total[3 * bands, : n + 1] / counts
    return (recon, bits, loss_terms, grad)


def solution(mesh):
    both = P("lat", "lon")
    return jax.shard_map(
        local,
        mesh=mesh,
        in_specs=(P(None, "lat", "lon"),) + (both,) * 7 + (P(),) * 10,
        out_specs=(P(None, "lat", "lon"), both, P(), P()),
        check_vma=False,
    )
```

```python
import functools

import jax
import jax.numpy as jnp
from jax import lax
from jax.experimental import pallas as pl
from jax.experimental.pallas import tpu as pltpu
from jax.sharding import PartitionSpec as P

mix_level = 668265263
mix_row = 374761393
mix_col = 1103515245
mix_mult = 73244475
log_two = 0.6931471805599453
context_steps = (
    (-1, 0),
    (1, 0),
    (0, -1),
    (0, 1),
    (-2, -1),
    (-2, 1),
    (2, -1),
    (2, 1),
    (-1, -2),
    (-1, 2),
    (1, -2),
    (1, 2),
)
MESH = pl.DeviceIdType.MESH
BF = jnp.bfloat16
F32 = jnp.float32
LANES = 128
SUB = 8


def width_of(cols):
    return cols + LANES if cols >= LANES else LANES


def iota(shape, dim):
    return lax.broadcasted_iota(jnp.int32, shape, dim)


def hashed_noise(seed_value, level_index, shape):
    value = seed_value + jnp.int32(level_index * mix_level % (1 << 32) - (1 << 32) * ((level_index * mix_level % (1 << 32)) >> 31))
    value = value + iota(shape, 0) * jnp.int32(mix_row) + iota(shape, 1) * jnp.int32(mix_col)
    value = value ^ lax.shift_right_logical(value, jnp.full(shape, 15, jnp.int32))
    value = value * jnp.int32(mix_mult)
    value = value ^ lax.shift_right_logical(value, jnp.full(shape, 13, jnp.int32))
    value = value * jnp.int32(mix_mult)
    value = value ^ lax.shift_right_logical(value, jnp.full(shape, 16, jnp.int32))
    return (value & jnp.int32(16777215)).astype(F32) / 16777216.0 - 0.5


def halo_kernel(shapes, seed_ref, *refs):
    n = len(shapes)
    latents, ext = refs[:n], refs[n : 2 * n]
    send_l, send_r, recv_r, recv_l, send_u, send_d, recv_b, recv_t, ssem, rsem = refs[2 * n :]
    lat, lon = lax.axis_index("lat"), lax.axis_index("lon")
    lats, lons = lax.axis_size("lat"), lax.axis_size("lon")
    left, right = (lat, lax.rem(lon + lons - 1, lons)), (lat, lax.rem(lon + 1, lons))
    up, down = (lax.rem(lat + lats - 1, lats), lon), (lax.rem(lat + 1, lats), lon)
    barrier = pltpu.get_barrier_semaphore()
    for other in (left, right, up, down):
        pl.semaphore_signal(barrier, inc=1, device_id=other, device_id_type=MESH)
    seed = seed_ref[0, 0]
    row = 0
    for level, (rows, cols) in enumerate(shapes):
        e = ext[level]
        tall = max(rows, SUB)
        e[...] = jnp.zeros_like(e)
        e[SUB : SUB + rows, 0:cols] = latents[level][...] + hashed_noise(seed, level, (rows, cols))
        if cols >= LANES:
            send_l[row : row + tall, :] = e[SUB : SUB + tall, 0:LANES]
            send_r[row : row + tall, :] = e[SUB : SUB + tall, cols - LANES : cols]
        else:
            whole = e[SUB : SUB + tall, :]
            send_l[row : row + tall, :] = whole
            send_r[row : row + tall, :] = pltpu.roll(whole, LANES - cols, 1)
        row += tall
    pl.semaphore_wait(barrier, 4)

    def copy(src, dst, index, other):
        return pltpu.make_async_remote_copy(
            src_ref=src,
            dst_ref=dst,
            send_sem=ssem.at[index],
            recv_sem=rsem.at[index],
            device_id=other,
            device_id_type=MESH,
        )

    to_left = copy(send_l, recv_r, 0, left)
    to_right = copy(send_r, recv_l, 1, right)
    to_left.start()
    to_right.start()
    to_left.wait()
    to_right.wait()
    row = 0
    lane0 = 0
    for level, (rows, cols) in enumerate(shapes):
        e = ext[level]
        tall = max(rows, SUB)
        from_right = recv_r[row : row + tall, :]
        from_left = recv_l[row : row + tall, :]
        lane = iota((tall, LANES), 1)
        if cols >= LANES:
            e[SUB : SUB + tall, cols : cols + LANES] = jnp.where(
                lane < LANES // 2, from_right, from_left
            )
        else:
            whole = e[SUB : SUB + tall, :]
            moved = pltpu.roll(from_right, cols, 1)
            halo = jnp.where(
                lane < cols + 4, moved, jnp.where(lane >= LANES - 4, from_left, 0.0)
            )
            e[SUB : SUB + tall, :] = jnp.where(lane < cols, whole, halo)
        wide = width_of(cols)
        send_u[:, lane0 : lane0 + wide] = e[SUB : 2 * SUB, :]
        send_d[:, lane0 : lane0 + wide] = e[tall : tall + SUB, :]
        row += tall
        lane0 += wide
    to_up = copy(send_u, recv_b, 2, up)
    to_down = copy(send_d, recv_t, 3, down)
    to_up.start()
    to_down.start()
    to_up.wait()
    to_down.wait()
    keep_t = jnp.where(lat > 0, 1.0, 0.0).astype(F32)
    keep_b = jnp.where(lat < lats - 1, 1.0, 0.0).astype(F32)
    lane0 = 0
    for level, (rows, cols) in enumerate(shapes):
        e = ext[level]
        wide = width_of(cols)
        top = recv_t[:, lane0 : lane0 + wide] * keep_t
        bottom = recv_b[:, lane0 : lane0 + wide] * keep_b
        reach = min(rows, SUB)
        e[SUB - reach : SUB, :] = top[:reach]
        e[SUB + rows : SUB + rows + reach, :] = bottom[:reach]
        lane0 += wide


def sum_kernel(part, total, row, col, send_sem, recv_sem):
    place = {"lon": lax.axis_index("lon"), "lat": lax.axis_index("lat")}
    barrier = pltpu.get_barrier_semaphore()

    def peers(axis):
        size = lax.axis_size(axis)
        for d in range(1, size):
            yield d - 1, {**place, axis: lax.rem(place[axis] + d, size)}

    count = 0
    for axis in ("lon", "lat"):
        for _, other in peers(axis):
            pl.semaphore_signal(
                barrier, inc=1, device_id=(other["lat"], other["lon"]), device_id_type=MESH
            )
            count += 1
    row[place["lon"]] = part[...]
    pl.semaphore_wait(barrier, count)
    first = 0
    for axis, slots in (("lon", row), ("lat", col)):
        mine = slots.at[place[axis]]
        copies = [
            pltpu.make_async_remote_copy(
                src_ref=mine,
                dst_ref=mine,
                send_sem=send_sem.at[first + d],
                recv_sem=recv_sem.at[first + d],
                device_id=(other["lat"], other["lon"]),
                device_id_type=MESH,
            )
            for d, other in peers(axis)
        ]
        for copy in copies:
            copy.start()
        for copy in copies:
            copy.wait()
        first += len(copies)
        added = slots[0]
        for d in range(1, lax.axis_size(axis)):
            added = added + slots[d]
        if axis == "lon":
            col[place["lat"]] = added
        else:
            total[...] = added


def dot(a, b):
    return jnp.dot(a, b, preferred_element_type=F32)


def parts(x, count):
    out = []
    for _ in range(count):
        piece = x.astype(BF)
        out.append(piece)
        x = x - piece.astype(F32)
    return out


def dot_pairs(a, x):
    hi, lo = parts(x, 2)
    return dot(a[0], hi) + (dot(a[1], hi) + dot(a[0], lo))


def div_24(x):
    return (x * 2731) >> 16


def looped(count, most, body, carry):
    each = next(k for k in range(min(most, count), 0, -1) if count % k == 0)

    def turn(t, carry):
        for k in range(each):
            carry = body(t * each + k, carry)
        return carry

    if each == count:
        return turn(0, carry)
    return lax.fori_loop(0, count // each, turn, carry)


def aligned(value, by):
    return value if isinstance(value, int) else pl.multiple_of(value, by)


def one_hot(flag):
    return jnp.where(flag, 1.0, 0.0).astype(BF)


def laplace_bits(offset, spread):
    magnitude = jnp.abs(offset)
    t = 1.0 / spread
    series = t * (1.0 - t * (0.5 - t * (1.0 / 6 - t * (1.0 / 24 - t * (1.0 / 120)))))
    gap = jnp.where(t < 0.1, series, 1.0 - jnp.exp(-t))
    outer = -log_two - (jnp.maximum(magnitude, 0.5) - 0.5) / spread + jnp.log(gap)
    inner_offset = jnp.clip(offset, -0.5, 0.5)
    inner = jnp.log(
        1.0
        - 0.5 * (jnp.exp(-(0.5 - inner_offset) / spread) + jnp.exp(-(0.5 + inner_offset) / spread))
    )
    return jnp.where(magnitude >= 0.5, outer, inner) * (-1.0 / log_two)


def local_kernel(shapes, ch, bands, pixel_count, *refs):
    n = len(shapes)
    ext = refs[:n]
    (
        target, parity, anchor, mix_l, mix_h, taps, c_in, c_mid, c_out,
        recon, bits_out, part, ups, second, third, fourth,
    ) = refs[n:]
    lat, lon = lax.axis_index("lat"), lax.axis_index("lon")
    lats = lax.axis_size("lat")
    rows_dev, cols_dev = shapes[0]
    wide = width_of(cols_dev)
    deep = SUB * ch
    reach = (SUB + 2) * ch
    stride = taps.shape[0] // 9

    lane_ch = iota((ch, deep), 1)
    fold = one_hot(lane_ch - ch * div_24(lane_ch) == iota((ch, deep), 0))
    same_row = div_24(iota((deep, deep), 0)) == div_24(iota((deep, deep), 1))

    def block_diagonal(w):
        return jnp.where(same_row, jnp.concatenate([dot(w, fold)] * SUB, 0), 0.0).astype(BF)

    def row_inside(w):
        k = w.shape[1]
        spread = one_hot((iota((k, k * SUB), 1) >> 3) == iota((k, k * SUB), 0))
        shape = (deep, k * SUB)
        keep = (iota(shape, 1) & 7) == div_24(iota(shape, 0))
        return jnp.where(keep, jnp.concatenate([dot(w, spread)] * SUB, 0), 0.0).astype(BF)

    def rows_out(w):
        wide_w = dot(w, fold)
        grown = jnp.concatenate(
            [jnp.broadcast_to(wide_w[o : o + 1], (SUB, deep)) for o in range(w.shape[0])], 0
        )
        shape = (w.shape[0] * SUB, deep)
        keep = (iota(shape, 0) & 7) == div_24(iota(shape, 1))
        return jnp.where(keep, grown, 0.0).astype(BF)

    t_levels = row_inside(mix_l[...])
    t_hidden = block_diagonal(mix_h[...])
    a_in = [row_inside(p) for p in parts(c_in[...], 2)]
    a_mid = [block_diagonal(p) for p in parts(c_mid[...], 2)]
    a_out = [rows_out(p) for p in parts(c_out[...], 2)]

    lane_re = iota((ch, reach), 1)
    fold_re = one_hot(lane_re - ch * div_24(lane_re) == iota((ch, reach), 0))
    wide_taps = dot(taps[...], fold_re)
    step = div_24(iota((deep, reach), 1)) - div_24(iota((deep, reach), 0))
    step_out = div_24(iota((bands * SUB, reach), 1)) - (iota((bands * SUB, reach), 0) & 7)

    def conv_taps(first_row):
        out = []
        for b in range(3):
            total = jnp.zeros((deep, reach), F32)
            for a in range(3):
                at = (3 * a + b) * stride + first_row
                total = jnp.where(
                    step == a, jnp.concatenate([wide_taps[at : at + ch]] * SUB, 0), total
                )
            out.append(total.astype(BF))
        return jnp.concatenate(out, 0)

    def output_taps():
        out = []
        for b in range(3):
            total = jnp.zeros((bands * SUB, reach), F32)
            for a in range(3):
                at = (3 * a + b) * stride + 2 * ch
                grown = jnp.concatenate(
                    [
                        jnp.broadcast_to(wide_taps[at + o : at + o + 1], (SUB, reach))
                        for o in range(bands)
                    ],
                    0,
                )
                total = jnp.where(step_out == a, grown, total)
            out.append(total)
        return jnp.concatenate(out, 0).astype(BF)

    t_first = conv_taps(0)
    t_second = conv_taps(ch)
    t_output = output_taps()

    tall_up = ups.shape[1]
    ups[0] = ext[0][SUB - 3 : SUB - 3 + tall_up, :]
    for level in range(1, n):
        rows, cols = shapes[level]
        e = ext[level]
        scale = 2.0 ** -level
        shape = (tall_up, e.shape[0])
        where_to = ((iota(shape, 0) - 3).astype(F32) + 0.5) * scale - 0.5
        along = jnp.maximum(
            0.0, 1.0 - jnp.abs(where_to - (iota(shape, 1) - SUB).astype(F32))
        ).astype(BF)
        hi, mid, lo = [dot(along, p) for p in parts(e[...], 3)]
        grown = hi + (mid + lo)
        shape = (e.shape[1], wide)
        pixel = iota(shape, 1)
        pixel = jnp.where(pixel < cols_dev + LANES // 2, pixel, pixel - wide)
        cell = iota(shape, 0)
        cell = jnp.where(cell < (cols + e.shape[1]) // 2, cell, cell - e.shape[1])
        where_to = (pixel.astype(F32) + 0.5) * scale - 0.5
        along = jnp.maximum(0.0, 1.0 - jnp.abs(where_to - cell.astype(F32))).astype(BF)
        hi, mid, lo = [dot(p, along) for p in parts(grown, 3)]
        ups[level] = hi + (mid + lo)

    def inside(field, start, margin):
        index = iota(field.shape, 0)
        begin = margin - start - lat * rows_dev
        keep = (index >= begin * ch) & (index < (begin + rows_dev * lats) * ch)
        return jnp.where(keep, field, 0.0)

    def mix_step(g, carry):
        here = pl.ds(aligned(g * SUB, SUB), SUB)
        x = jnp.concatenate([ups[level, here, :] for level in range(n)], 0).astype(BF)
        f = jnp.maximum(dot(t_levels, x), 0.0).astype(BF)
        s = jnp.maximum(dot(t_hidden, f), 0.0)
        second[pl.ds(aligned(g * deep, deep), deep), :] = inside(s, g * SUB, 3).astype(BF)
        return carry

    looped(tall_up // SUB, 3, mix_step, 0)

    def conv_pass(src, dst, weights, count, margin):
        def step_fn(k, carry):
            start = min(k * SUB, count - SUB) if isinstance(k, int) else jnp.minimum(k * SUB, count - SUB)
            at = aligned(start * ch, 2 * ch)
            x = src[pl.ds(at, reach), :]
            p = dot(weights, x)
            c = (
                p[deep : 2 * deep]
                + pltpu.roll(p[:deep], 1, 1)
                + pltpu.roll(p[2 * deep :], wide - 1, 1)
            )
            r = x.astype(F32)[ch : ch + deep] + jnp.maximum(c, 0.0)
            dst[pl.ds(at, deep), :] = inside(r, start, margin).astype(BF)
            return carry

        looped((count + SUB - 1) // SUB, 3, step_fn, 0)

    conv_pass(second, third, t_first, rows_dev + 4, 2)
    conv_pass(third, fourth, t_second, rows_dev + 2, 1)

    def output_step(k, carry):
        squares, grad = carry
        x = fourth[pl.ds(aligned(k * deep, deep), reach), :]
        p = dot(t_output, x)
        m = bands * SUB
        c = p[m : 2 * m] + pltpu.roll(p[:m], 1, 1) + pltpu.roll(p[2 * m :], wide - 1, 1)
        c = c[:, :cols_dev]
        here = pl.ds(aligned(k * SUB, SUB), SUB)
        for o in range(bands):
            recon[o, here, :] = c[o * SUB : (o + 1) * SUB]
        error = c - jnp.concatenate([target[o, here, :] for o in range(bands)], 0)
        slope = (2.0 * error / pixel_count).astype(BF).astype(F32)
        slope = jnp.concatenate([slope, jnp.zeros((m, wide - cols_dev), F32)], 1)
        slopes = jnp.concatenate(
            [pltpu.roll(slope, wide - 1, 1), slope, pltpu.roll(slope, 1, 1)], 0
        ).astype(BF)
        grad = grad + lax.dot_general(
            slopes, x, (((1,), (1,)), ((), ())), preferred_element_type=F32
        )
        return squares + error * error, grad

    m = bands * SUB
    squares, grad = looped(
        rows_dev // SUB,
        4,
        output_step,
        (jnp.zeros((m, cols_dev), F32), jnp.zeros((3 * m, reach), F32)),
    )
    pad = -reach % LANES
    grad = jnp.concatenate([grad, jnp.zeros((3 * m, pad), F32)], 1)
    line = iota(grad.shape, 0) & 7
    moved = grad
    for y in range(1, SUB):
        moved = jnp.where(line == y, pltpu.roll(grad, reach + pad - y * ch, 1), moved)
    folded = jnp.sum(moved[:, :LANES].reshape(3 * bands, SUB, LANES), axis=1)
    sums = jnp.concatenate([folded, jnp.zeros((part.shape[0] - 3 * bands, LANES), F32)], 0)

    shape = part.shape
    last = iota(shape, 0) == 3 * bands

    def put(sums, lane, value):
        return jnp.where(last & (iota(shape, 1) == lane), value, sums)

    sums = put(sums, 0, jnp.sum(squares))

    for level, (rows, cols) in enumerate(shapes):
        e = ext[level]
        cover = max(cols, LANES)
        full = e.shape[1]
        scale = anchor[level]
        odd = lat * rows + lon * cols + parity[level]

        def rate_step(g, total, level=level, rows=rows, cols=cols, e=e, cover=cover, full=full, scale=scale, odd=odd):
            window = e[pl.ds(aligned(g * SUB, SUB), 3 * SUB), :]
            moved = {i: window[SUB + i : 2 * SUB + i] for i in range(-2, 3)}
            context = [
                (moved[i] if j == 0 else pltpu.roll(moved[i], (-j) % full, 1))[:, :cover]
                for i, j in context_steps
            ]
            inner = jnp.maximum(dot_pairs(a_in, jnp.concatenate(context, 0)), 0.0)
            outer = jnp.maximum(dot_pairs(a_mid, inner), 0.0)
            raw = dot_pairs(a_out, outer)
            mu, sigma = raw[:SUB], raw[SUB:]
            row, col = iota((SUB, cover), 0), iota((SUB, cover), 1)
            first = ((row + col + odd) & 1) == 0
            centre = jnp.where(first, 0.0, mu)
            soft = jnp.maximum(sigma, 0.0) + jnp.log1p(jnp.exp(-jnp.abs(sigma)))
            spread = jnp.where(first, scale, 0.1 + soft)
            bits = laplace_bits(moved[0][:, :cover] - centre, spread)
            if level == 0:
                bits_out[pl.ds(aligned(g * SUB, SUB), SUB), :] = bits
            if rows < SUB or cols < LANES:
                bits = jnp.where((row < rows) & (col < cols), bits, 0.0)
            return total + bits

        total = looped(max(1, rows // SUB), 4, rate_step, jnp.zeros((SUB, cover), F32))
        sums = put(sums, 1 + level, jnp.sum(total))
    part[...] = sums


def local(target, *args):
    latents = args[:-11]
    (
        tile_seeds, anchor_parity, anchor_scale, mix_levels, mix_hidden,
        conv_first, conv_second, conv_output, context_in, context_mid, context_out,
    ) = args[-11:]
    n = len(latents)
    shapes = [x.shape for x in latents]
    bands, rows_dev, cols_dev = target.shape
    ch = mix_hidden.shape[0]
    devices = lax.axis_size("lat") * lax.axis_size("lon")
    pixel_count = float(bands * rows_dev * cols_dev * devices)
    vmem = pl.BlockSpec(memory_space=pltpu.VMEM)
    smem = pl.BlockSpec(memory_space=pltpu.SMEM)
    wides = [width_of(c) for _, c in shapes]
    talls = [max(r, SUB) for r, _ in shapes]
    edge = pltpu.VMEM((sum(talls), LANES), F32)
    belt = pltpu.VMEM((SUB, sum(wides)), F32)
    extended = pl.pallas_call(
        functools.partial(halo_kernel, shapes),
        out_shape=[
            jax.ShapeDtypeStruct((t + 2 * SUB, w), F32) for t, w in zip(talls, wides)
        ],
        in_specs=[smem] + [vmem] * n,
        out_specs=[vmem] * n,
        scratch_shapes=[edge] * 4
        + [belt] * 4
        + [pltpu.SemaphoreType.DMA((4,)), pltpu.SemaphoreType.DMA((4,))],
        compiler_params=pltpu.CompilerParams(
            collective_id=0, has_side_effects=True, vmem_limit_bytes=16 * 2**20
        ),
        name="halo",
    )(tile_seeds, *latents)
    taps = jnp.concatenate([conv_first, conv_second, conv_output], 0).transpose(2, 3, 0, 1)
    taps = jnp.pad(taps, ((0, 0), (0, 0), (0, -taps.shape[2] % SUB), (0, 0))).reshape(-1, ch)
    wide = wides[0]
    tall_up = rows_dev + SUB
    recon, bits, part = pl.pallas_call(
        functools.partial(local_kernel, shapes, ch, bands, pixel_count),
        out_shape=[
            jax.ShapeDtypeStruct(target.shape, F32),
            jax.ShapeDtypeStruct((rows_dev, cols_dev), F32),
            jax.ShapeDtypeStruct((2 * SUB, LANES), F32),
        ],
        in_specs=[vmem] * (n + 1) + [smem] * 2 + [vmem] * 6,
        out_specs=[vmem] * 3,
        scratch_shapes=[
            pltpu.VMEM((n, tall_up, wide), F32),
            pltpu.VMEM((tall_up * ch, wide), BF),
            pltpu.VMEM(((rows_dev + 4) * ch, wide), BF),
            pltpu.VMEM(((rows_dev + 2) * ch, wide), BF),
        ],
        compiler_params=pltpu.CompilerParams(vmem_limit_bytes=48 * 2**20),
        name="step",
    )(
        *extended, target, anchor_parity, anchor_scale, mix_levels, mix_hidden,
        taps, context_in, context_mid, context_out,
    )
    lats, lons = lax.axis_size("lat"), lax.axis_size("lon")
    total = pl.pallas_call(
        sum_kernel,
        out_shape=jax.ShapeDtypeStruct(part.shape, F32),
        in_specs=[vmem],
        out_specs=vmem,
        scratch_shapes=[
            pltpu.VMEM((lons,) + part.shape, F32),
            pltpu.VMEM((lats,) + part.shape, F32),
            pltpu.SemaphoreType.DMA((lats + lons - 2,)),
            pltpu.SemaphoreType.DMA((lats + lons - 2,)),
        ],
        compiler_params=pltpu.CompilerParams(
            collective_id=1, has_side_effects=True, vmem_limit_bytes=8 * 2**20
        ),
        name="sums",
    )(part)
    grad = total[: 3 * bands, : 3 * ch].reshape(3, bands, 3, ch).transpose(1, 3, 2, 0)
    counts = jnp.array(
        [pixel_count] + [float(r * c * devices) for r, c in shapes], dtype=F32
    )
    loss_terms = total[3 * bands, : n + 1] / counts
    return (recon, bits, loss_terms, grad)


def solution(mesh):
    both = P("lat", "lon")
    return jax.shard_map(
        local,
        mesh=mesh,
        in_specs=(P(None, "lat", "lon"),) + (both,) * 7 + (P(),) * 10,
        out_specs=(P(None, "lat", "lon"), both, P(), P()),
        check_vma=False,
    )
```

```python
import functools

import jax
import jax.numpy as jnp
from jax import lax
from jax.experimental import pallas as pl
from jax.experimental.pallas import tpu as pltpu
from jax.sharding import PartitionSpec as P

mix_level = 668265263
mix_row = 374761393
mix_col = 1103515245
mix_mult = 73244475
log_two = 0.6931471805599453
context_steps = (
    (-1, 0),
    (1, 0),
    (0, -1),
    (0, 1),
    (-2, -1),
    (-2, 1),
    (2, -1),
    (2, 1),
    (-1, -2),
    (-1, 2),
    (1, -2),
    (1, 2),
)
MESH = pl.DeviceIdType.MESH
BF = jnp.bfloat16
F32 = jnp.float32
LANES = 128
SUB = 8


def width_of(cols):
    return cols + LANES if cols >= LANES else LANES


def iota(shape, dim):
    return lax.broadcasted_iota(jnp.int32, shape, dim)


def hashed_noise(seed_value, level_index, shape):
    value = seed_value + jnp.int32(level_index * mix_level % (1 << 32) - (1 << 32) * ((level_index * mix_level % (1 << 32)) >> 31))
    value = value + iota(shape, 0) * jnp.int32(mix_row) + iota(shape, 1) * jnp.int32(mix_col)
    value = value ^ lax.shift_right_logical(value, jnp.full(shape, 15, jnp.int32))
    value = value * jnp.int32(mix_mult)
    value = value ^ lax.shift_right_logical(value, jnp.full(shape, 13, jnp.int32))
    value = value * jnp.int32(mix_mult)
    value = value ^ lax.shift_right_logical(value, jnp.full(shape, 16, jnp.int32))
    return (value & jnp.int32(16777215)).astype(F32) / 16777216.0 - 0.5


def halo_kernel(shapes, seed_ref, *refs):
    n = len(shapes)
    latents, ext = refs[:n], refs[n : 2 * n]
    send_l, send_r, recv_r, recv_l, send_u, send_d, recv_b, recv_t, ssem, rsem = refs[2 * n :]
    lat, lon = lax.axis_index("lat"), lax.axis_index("lon")
    lats, lons = lax.axis_size("lat"), lax.axis_size("lon")
    left, right = (lat, lax.rem(lon + lons - 1, lons)), (lat, lax.rem(lon + 1, lons))
    up, down = (lax.rem(lat + lats - 1, lats), lon), (lax.rem(lat + 1, lats), lon)
    barrier = pltpu.get_barrier_semaphore()
    for other in (left, right, up, down):
        pl.semaphore_signal(barrier, inc=1, device_id=other, device_id_type=MESH)
    seed = seed_ref[0, 0]
    row = 0
    for level, (rows, cols) in enumerate(shapes):
        e = ext[level]
        tall = max(rows, SUB)
        e[...] = jnp.zeros_like(e)
        e[SUB : SUB + rows, 0:cols] = latents[level][...] + hashed_noise(seed, level, (rows, cols))
        if cols >= LANES:
            send_l[row : row + tall, :] = e[SUB : SUB + tall, 0:LANES]
            send_r[row : row + tall, :] = e[SUB : SUB + tall, cols - LANES : cols]
        else:
            whole = e[SUB : SUB + tall, :]
            send_l[row : row + tall, :] = whole
            send_r[row : row + tall, :] = pltpu.roll(whole, LANES - cols, 1)
        row += tall
    pl.semaphore_wait(barrier, 4)

    def copy(src, dst, index, other):
        return pltpu.make_async_remote_copy(
            src_ref=src,
            dst_ref=dst,
            send_sem=ssem.at[index],
            recv_sem=rsem.at[index],
            device_id=other,
            device_id_type=MESH,
        )

    to_left = copy(send_l, recv_r, 0, left)
    to_right = copy(send_r, recv_l, 1, right)
    to_left.start()
    to_right.start()
    to_left.wait()
    to_right.wait()
    row = 0
    lane0 = 0
    for level, (rows, cols) in enumerate(shapes):
        e = ext[level]
        tall = max(rows, SUB)
        from_right = recv_r[row : row + tall, :]
        from_left = recv_l[row : row + tall, :]
        lane = iota((tall, LANES), 1)
        if cols >= LANES:
            e[SUB : SUB + tall, cols : cols + LANES] = jnp.where(
                lane < LANES // 2, from_right, from_left
            )
        else:
            whole = e[SUB : SUB + tall, :]
            moved = pltpu.roll(from_right, cols, 1)
            halo = jnp.where(
                lane < cols + 4, moved, jnp.where(lane >= LANES - 4, from_left, 0.0)
            )
            e[SUB : SUB + tall, :] = jnp.where(lane < cols, whole, halo)
        wide = width_of(cols)
        send_u[:, lane0 : lane0 + wide] = e[SUB : 2 * SUB, :]
        send_d[:, lane0 : lane0 + wide] = e[tall : tall + SUB, :]
        row += tall
        lane0 += wide
    to_up = copy(send_u, recv_b, 2, up)
    to_down = copy(send_d, recv_t, 3, down)
    to_up.start()
    to_down.start()
    to_up.wait()
    to_down.wait()
    keep_t = jnp.where(lat > 0, 1.0, 0.0).astype(F32)
    keep_b = jnp.where(lat < lats - 1, 1.0, 0.0).astype(F32)
    lane0 = 0
    for level, (rows, cols) in enumerate(shapes):
        e = ext[level]
        wide = width_of(cols)
        top = recv_t[:, lane0 : lane0 + wide] * keep_t
        bottom = recv_b[:, lane0 : lane0 + wide] * keep_b
        reach = min(rows, SUB)
        e[SUB - reach : SUB, :] = top[:reach]
        e[SUB + rows : SUB + rows + reach, :] = bottom[:reach]
        lane0 += wide


def sum_kernel(part, total, row, col, send_sem, recv_sem):
    place = {"lon": lax.axis_index("lon"), "lat": lax.axis_index("lat")}
    barrier = pltpu.get_barrier_semaphore()

    def peers(axis):
        size = lax.axis_size(axis)
        for d in range(1, size):
            yield d - 1, {**place, axis: lax.rem(place[axis] + d, size)}

    count = 0
    for axis in ("lon", "lat"):
        for _, other in peers(axis):
            pl.semaphore_signal(
                barrier, inc=1, device_id=(other["lat"], other["lon"]), device_id_type=MESH
            )
            count += 1
    row[place["lon"]] = part[...]
    pl.semaphore_wait(barrier, count)
    first = 0
    for axis, slots in (("lon", row), ("lat", col)):
        mine = slots.at[place[axis]]
        copies = [
            pltpu.make_async_remote_copy(
                src_ref=mine,
                dst_ref=mine,
                send_sem=send_sem.at[first + d],
                recv_sem=recv_sem.at[first + d],
                device_id=(other["lat"], other["lon"]),
                device_id_type=MESH,
            )
            for d, other in peers(axis)
        ]
        for copy in copies:
            copy.start()
        for copy in copies:
            copy.wait()
        first += len(copies)
        added = slots[0]
        for d in range(1, lax.axis_size(axis)):
            added = added + slots[d]
        if axis == "lon":
            col[place["lat"]] = added
        else:
            total[...] = added


def dot(a, b):
    return jnp.dot(a, b, preferred_element_type=F32)


def parts(x, count):
    out = []
    for _ in range(count):
        piece = x.astype(BF)
        out.append(piece)
        x = x - piece.astype(F32)
    return out


def dot_pairs(a, x):
    hi, lo = parts(x, 2)
    m, k = a.shape[0] // 2, a.shape[1]
    if k == 2 * x.shape[0]:
        p = dot(a, jnp.concatenate([hi, lo], 0))
        return p[:m] + p[m:]
    p = dot(a, hi)
    return p[:m] + (p[m:] + dot(a[:m], lo))


def div_24(x):
    return (x * 2731) >> 16


def looped(count, most, body, carry):
    each = next(k for k in range(min(most, count), 0, -1) if count % k == 0)

    def turn(t, carry):
        for k in range(each):
            carry = body(t * each + k, carry)
        return carry

    if each == count:
        return turn(0, carry)
    return lax.fori_loop(0, count // each, turn, carry)


def aligned(value, by):
    return value if isinstance(value, int) else pl.multiple_of(value, by)


def one_hot(flag):
    return jnp.where(flag, 1.0, 0.0).astype(BF)


def laplace_bits(offset, spread):
    magnitude = jnp.abs(offset)
    t = 1.0 / spread
    series = t * (1.0 - t * (0.5 - t * (1.0 / 6 - t * (1.0 / 24 - t * (1.0 / 120)))))
    gap = jnp.where(t < 0.1, series, 1.0 - jnp.exp(-t))
    outer = -log_two - (jnp.maximum(magnitude, 0.5) - 0.5) / spread + jnp.log(gap)
    inner_offset = jnp.clip(offset, -0.5, 0.5)
    inner = jnp.log(
        1.0
        - 0.5 * (jnp.exp(-(0.5 - inner_offset) / spread) + jnp.exp(-(0.5 + inner_offset) / spread))
    )
    return jnp.where(magnitude >= 0.5, outer, inner) * (-1.0 / log_two)


def local_kernel(shapes, ch, bands, pixel_count, *refs):
    n = len(shapes)
    ext = refs[:n]
    (
        target, parity, anchor, mix_l, mix_h, w_first, w_second, w_output, c_in, c_mid, c_out,
        recon, bits_out, part, ups, second, third, fourth,
    ) = refs[n:]
    lat, lon = lax.axis_index("lat"), lax.axis_index("lon")
    lats = lax.axis_size("lat")
    rows_dev, cols_dev = shapes[0]
    wide = width_of(cols_dev)
    deep = SUB * ch
    reach = (SUB + 2) * ch

    lane_ch = iota((ch, deep), 1)
    fold = one_hot(lane_ch - ch * div_24(lane_ch) == iota((ch, deep), 0))
    same_row = div_24(iota((deep, deep), 0)) == div_24(iota((deep, deep), 1))

    def block_diagonal(w):
        return jnp.where(same_row, jnp.concatenate([dot(w, fold)] * SUB, 0), 0.0).astype(BF)

    def row_inside(w):
        k = w.shape[1]
        spread = one_hot((iota((k, k * SUB), 1) >> 3) == iota((k, k * SUB), 0))
        shape = (deep, k * SUB)
        keep = (iota(shape, 1) & 7) == div_24(iota(shape, 0))
        return jnp.where(keep, jnp.concatenate([dot(w, spread)] * SUB, 0), 0.0).astype(BF)

    def rows_out(w):
        wide_w = dot(w, fold)
        grown = jnp.concatenate(
            [jnp.broadcast_to(wide_w[o : o + 1], (SUB, deep)) for o in range(w.shape[0])], 0
        )
        shape = (w.shape[0] * SUB, deep)
        keep = (iota(shape, 0) & 7) == div_24(iota(shape, 1))
        return jnp.where(keep, grown, 0.0).astype(BF)

    t_levels = row_inside(mix_l[...])
    t_hidden = block_diagonal(mix_h[...])
    a_in = jnp.concatenate([row_inside(p) for p in parts(c_in[...], 2)], 0)
    a_in = jnp.concatenate([a_in, a_in], 1)
    a_mid = jnp.concatenate([block_diagonal(p) for p in parts(c_mid[...], 2)], 0)
    a_out = jnp.concatenate([rows_out(p) for p in parts(c_out[...], 2)], 0)

    lane_re = iota((ch, reach), 1)
    fold_re = one_hot(lane_re - ch * div_24(lane_re) == iota((ch, reach), 0))
    step = div_24(iota((deep, reach), 1)) - div_24(iota((deep, reach), 0))
    step_out = div_24(iota((bands * SUB, reach), 1)) - (iota((bands * SUB, reach), 0) & 7)

    def conv_taps(w):
        grown = [[dot(w[a, b], fold_re) for b in range(3)] for a in range(3)]
        out = []
        for b in range(3):
            total = jnp.zeros((deep, reach), F32)
            for a in range(3):
                total = jnp.where(step == a, jnp.concatenate([grown[a][b]] * SUB, 0), total)
            out.append(total.astype(BF))
        return jnp.concatenate(out, 0)

    def output_taps():
        out = []
        for b in range(3):
            total = jnp.zeros((bands * SUB, reach), F32)
            for a in range(3):
                one = dot(w_output[a, b], fold_re)
                grown = jnp.concatenate(
                    [
                        jnp.broadcast_to(one[o : o + 1], (SUB, reach))
                        for o in range(bands)
                    ],
                    0,
                )
                total = jnp.where(step_out == a, grown, total)
            out.append(total)
        return jnp.concatenate(out, 0).astype(BF)

    t_first = conv_taps(w_first)
    t_second = conv_taps(w_second)
    t_output = output_taps()

    tall_up = ups.shape[1]
    ups[0] = ext[0][SUB - 3 : SUB - 3 + tall_up, :]
    for level in range(1, n):
        rows, cols = shapes[level]
        e = ext[level]
        scale = 2.0 ** -level
        shape = (tall_up, e.shape[0])
        where_to = ((iota(shape, 0) - 3).astype(F32) + 0.5) * scale - 0.5
        along = jnp.maximum(
            0.0, 1.0 - jnp.abs(where_to - (iota(shape, 1) - SUB).astype(F32))
        ).astype(BF)
        hi, mid, lo = [dot(along, p) for p in parts(e[...], 3)]
        grown = hi + (mid + lo)
        shape = (e.shape[1], wide)
        pixel = iota(shape, 1)
        pixel = jnp.where(pixel < cols_dev + LANES // 2, pixel, pixel - wide)
        cell = iota(shape, 0)
        cell = jnp.where(cell < (cols + e.shape[1]) // 2, cell, cell - e.shape[1])
        where_to = (pixel.astype(F32) + 0.5) * scale - 0.5
        along = jnp.maximum(0.0, 1.0 - jnp.abs(where_to - cell.astype(F32))).astype(BF)
        hi, mid, lo = [dot(p, along) for p in parts(grown, 3)]
        ups[level] = hi + (mid + lo)

    def inside(field, start, margin):
        index = iota(field.shape, 0)
        begin = margin - start - lat * rows_dev
        keep = (index >= begin * ch) & (index < (begin + rows_dev * lats) * ch)
        return jnp.where(keep, field, 0.0)

    def mix_step(g, carry):
        here = pl.ds(aligned(g * SUB, SUB), SUB)
        x = jnp.concatenate([ups[level, here, :] for level in range(n)], 0).astype(BF)
        f = jnp.maximum(dot(t_levels, x), 0.0).astype(BF)
        s = jnp.maximum(dot(t_hidden, f), 0.0)
        second[pl.ds(aligned(g * deep, deep), deep), :] = inside(s, g * SUB, 3).astype(BF)
        return carry

    looped(tall_up // SUB, 3, mix_step, 0)

    def conv_pass(src, dst, weights, count, margin):
        def step_fn(k, carry):
            start = min(k * SUB, count - SUB) if isinstance(k, int) else jnp.minimum(k * SUB, count - SUB)
            at = aligned(start * ch, 2 * ch)
            x = src[pl.ds(at, reach), :]
            p = dot(weights, x)
            c = (
                p[deep : 2 * deep]
                + pltpu.roll(p[:deep], 1, 1)
                + pltpu.roll(p[2 * deep :], wide - 1, 1)
            )
            r = x.astype(F32)[ch : ch + deep] + jnp.maximum(c, 0.0)
            dst[pl.ds(at, deep), :] = inside(r, start, margin).astype(BF)
            return carry

        looped((count + SUB - 1) // SUB, 3, step_fn, 0)

    conv_pass(second, third, t_first, rows_dev + 4, 2)
    conv_pass(third, fourth, t_second, rows_dev + 2, 1)

    def output_step(k, carry):
        squares, grad = carry
        x = fourth[pl.ds(aligned(k * deep, deep), reach), :]
        p = dot(t_output, x)
        m = bands * SUB
        c = p[m : 2 * m] + pltpu.roll(p[:m], 1, 1) + pltpu.roll(p[2 * m :], wide - 1, 1)
        c = c[:, :cols_dev]
        here = pl.ds(aligned(k * SUB, SUB), SUB)
        for o in range(bands):
            recon[o, here, :] = c[o * SUB : (o + 1) * SUB]
        error = c - jnp.concatenate([target[o, here, :] for o in range(bands)], 0)
        slope = (2.0 * error / pixel_count).astype(BF).astype(F32)
        slope = jnp.concatenate([slope, jnp.zeros((m, wide - cols_dev), F32)], 1)
        slopes = jnp.concatenate(
            [pltpu.roll(slope, wide - 1, 1), slope, pltpu.roll(slope, 1, 1)], 0
        ).astype(BF)
        grad = grad + lax.dot_general(
            slopes, x, (((1,), (1,)), ((), ())), preferred_element_type=F32
        )
        return squares + error * error, grad

    m = bands * SUB
    squares, grad = looped(
        rows_dev // SUB,
        4,
        output_step,
        (jnp.zeros((m, cols_dev), F32), jnp.zeros((3 * m, reach), F32)),
    )
    pad = -reach % LANES
    grad = jnp.concatenate([grad, jnp.zeros((3 * m, pad), F32)], 1)
    line = iota(grad.shape, 0) & 7
    moved = grad
    for y in range(1, SUB):
        moved = jnp.where(line == y, pltpu.roll(grad, reach + pad - y * ch, 1), moved)
    folded = jnp.sum(moved[:, :LANES].reshape(3 * bands, SUB, LANES), axis=1)
    sums = jnp.concatenate([folded, jnp.zeros((part.shape[0] - 3 * bands, LANES), F32)], 0)

    shape = part.shape
    last = iota(shape, 0) == 3 * bands

    def put(sums, lane, value):
        return jnp.where(last & (iota(shape, 1) == lane), value, sums)

    sums = put(sums, 0, jnp.sum(squares))

    for level, (rows, cols) in enumerate(shapes):
        e = ext[level]
        cover = max(cols, LANES)
        full = e.shape[1]
        scale = anchor[level]
        odd = lat * rows + lon * cols + parity[level]

        blocks = 2 if rows % (2 * SUB) == 0 else 1

        def rate_step(g, total, blocks=blocks, level=level, rows=rows, cols=cols, e=e, cover=cover, full=full, scale=scale, odd=odd):
            def context_of(block):
                window = e[pl.ds(aligned(block * SUB, SUB), 3 * SUB), :]
                moved = {i: window[SUB + i : 2 * SUB + i] for i in range(-2, 3)}
                near = [
                    (moved[i] if j == 0 else pltpu.roll(moved[i], (-j) % full, 1))[:, :cover]
                    for i, j in context_steps
                ]
                return near, moved[0][:, :cover]

            row, col = iota((SUB, cover), 0), iota((SUB, cover), 1)
            first = ((row + col + odd) & 1) == 0
            near, here = context_of(g * blocks)
            cells = [here]
            if blocks == 2:
                later, here = context_of(g * blocks + 1)
                cells.append(here)
                near = [
                    jnp.where(first, pltpu.roll(q, cover - 1, 1), p) for p, q in zip(near, later)
                ]
            inner = jnp.maximum(dot_pairs(a_in, jnp.concatenate(near, 0)), 0.0)
            outer = jnp.maximum(dot_pairs(a_mid, inner), 0.0)
            raw = dot_pairs(a_out, outer)
            mu, sigma = raw[:SUB], raw[SUB:]
            soft = 0.1 + jnp.maximum(sigma, 0.0) + jnp.log1p(jnp.exp(-jnp.abs(sigma)))
            for k, here in enumerate(cells):
                if k == 1:
                    mu, soft = pltpu.roll(mu, 1, 1), pltpu.roll(soft, 1, 1)
                centre = jnp.where(first, 0.0, mu)
                spread = jnp.where(first, scale, soft)
                bits = laplace_bits(here - centre, spread)
                if level == 0:
                    bits_out[pl.ds(aligned((g * blocks + k) * SUB, SUB), SUB), :] = bits
                if rows < SUB or cols < LANES:
                    bits = jnp.where((row < rows) & (col < cols), bits, 0.0)
                total = total + bits
            return total

        total = looped(max(1, rows // (SUB * blocks)), 2, rate_step, jnp.zeros((SUB, cover), F32))
        sums = put(sums, 1 + level, jnp.sum(total))
    part[...] = sums


def local(target, *args):
    latents = args[:-11]
    (
        tile_seeds, anchor_parity, anchor_scale, mix_levels, mix_hidden,
        conv_first, conv_second, conv_output, context_in, context_mid, context_out,
    ) = args[-11:]
    n = len(latents)
    shapes = [x.shape for x in latents]
    bands, rows_dev, cols_dev = target.shape
    ch = mix_hidden.shape[0]
    devices = lax.axis_size("lat") * lax.axis_size("lon")
    pixel_count = float(bands * rows_dev * cols_dev * devices)
    vmem = pl.BlockSpec(memory_space=pltpu.VMEM)
    smem = pl.BlockSpec(memory_space=pltpu.SMEM)
    wides = [width_of(c) for _, c in shapes]
    talls = [max(r, SUB) for r, _ in shapes]
    edge = pltpu.VMEM((sum(talls), LANES), F32)
    belt = pltpu.VMEM((SUB, sum(wides)), F32)
    extended = pl.pallas_call(
        functools.partial(halo_kernel, shapes),
        out_shape=[
            jax.ShapeDtypeStruct((t + 2 * SUB, w), F32) for t, w in zip(talls, wides)
        ],
        in_specs=[smem] + [vmem] * n,
        out_specs=[vmem] * n,
        scratch_shapes=[edge] * 4
        + [belt] * 4
        + [pltpu.SemaphoreType.DMA((4,)), pltpu.SemaphoreType.DMA((4,))],
        compiler_params=pltpu.CompilerParams(
            collective_id=0, has_side_effects=True, vmem_limit_bytes=16 * 2**20
        ),
        name="halo",
    )(tile_seeds, *latents)
    convs = [w.transpose(2, 3, 0, 1) for w in (conv_first, conv_second, conv_output)]
    wide = wides[0]
    tall_up = rows_dev + SUB
    recon, bits, part = pl.pallas_call(
        functools.partial(local_kernel, shapes, ch, bands, pixel_count),
        out_shape=[
            jax.ShapeDtypeStruct(target.shape, F32),
            jax.ShapeDtypeStruct((rows_dev, cols_dev), F32),
            jax.ShapeDtypeStruct((2 * SUB, LANES), F32),
        ],
        in_specs=[vmem] * (n + 1) + [smem] * 2 + [vmem] * 8,
        out_specs=[vmem] * 3,
        scratch_shapes=[
            pltpu.VMEM((n, tall_up, wide), F32),
            pltpu.VMEM((tall_up * ch, wide), BF),
            pltpu.VMEM(((rows_dev + 4) * ch, wide), BF),
            pltpu.VMEM(((rows_dev + 2) * ch, wide), BF),
        ],
        compiler_params=pltpu.CompilerParams(vmem_limit_bytes=48 * 2**20),
        name="step",
    )(
        *extended, target, anchor_parity, anchor_scale, mix_levels, mix_hidden,
        *convs, context_in, context_mid, context_out,
    )
    lats, lons = lax.axis_size("lat"), lax.axis_size("lon")
    total = pl.pallas_call(
        sum_kernel,
        out_shape=jax.ShapeDtypeStruct(part.shape, F32),
        in_specs=[vmem],
        out_specs=vmem,
        scratch_shapes=[
            pltpu.VMEM((lons,) + part.shape, F32),
            pltpu.VMEM((lats,) + part.shape, F32),
            pltpu.SemaphoreType.DMA((lats + lons - 2,)),
            pltpu.SemaphoreType.DMA((lats + lons - 2,)),
        ],
        compiler_params=pltpu.CompilerParams(
            collective_id=1, has_side_effects=True, vmem_limit_bytes=8 * 2**20
        ),
        name="sums",
    )(part)
    grad = total[: 3 * bands, : 3 * ch].reshape(3, bands, 3, ch).transpose(1, 3, 2, 0)
    counts = jnp.array(
        [pixel_count] + [float(r * c * devices) for r, c in shapes], dtype=F32
    )
    loss_terms = total[3 * bands, : n + 1] / counts
    return (recon, bits, loss_terms, grad)


def solution(mesh):
    both = P("lat", "lon")
    return jax.shard_map(
        local,
        mesh=mesh,
        in_specs=(P(None, "lat", "lon"),) + (both,) * 7 + (P(),) * 10,
        out_specs=(P(None, "lat", "lon"), both, P(), P()),
        check_vma=False,
    )
```

```python
import functools

import jax
import jax.numpy as jnp
from jax import lax
from jax.experimental import pallas as pl
from jax.experimental.pallas import tpu as pltpu
from jax.sharding import PartitionSpec as P

mix_level = 668265263
mix_row = 374761393
mix_col = 1103515245
mix_mult = 73244475
log_two = 0.6931471805599453
context_steps = (
    (-1, 0),
    (1, 0),
    (0, -1),
    (0, 1),
    (-2, -1),
    (-2, 1),
    (2, -1),
    (2, 1),
    (-1, -2),
    (-1, 2),
    (1, -2),
    (1, 2),
)
MESH = pl.DeviceIdType.MESH
BF = jnp.bfloat16
F32 = jnp.float32
LANES = 128
SUB = 8


def width_of(cols):
    return cols + LANES if cols >= LANES else LANES


def iota(shape, dim):
    return lax.broadcasted_iota(jnp.int32, shape, dim)


def hashed_noise(seed_value, level_index, shape):
    value = seed_value + jnp.int32(level_index * mix_level % (1 << 32) - (1 << 32) * ((level_index * mix_level % (1 << 32)) >> 31))
    value = value + iota(shape, 0) * jnp.int32(mix_row) + iota(shape, 1) * jnp.int32(mix_col)
    value = value ^ lax.shift_right_logical(value, jnp.full(shape, 15, jnp.int32))
    value = value * jnp.int32(mix_mult)
    value = value ^ lax.shift_right_logical(value, jnp.full(shape, 13, jnp.int32))
    value = value * jnp.int32(mix_mult)
    value = value ^ lax.shift_right_logical(value, jnp.full(shape, 16, jnp.int32))
    return (value & jnp.int32(16777215)).astype(F32) / 16777216.0 - 0.5


def halo_kernel(shapes, seed_ref, *refs):
    n = len(shapes)
    latents, ext = refs[:n], refs[n : 2 * n]
    send_l, send_r, recv_r, recv_l, send_u, send_d, recv_b, recv_t, ssem, rsem = refs[2 * n :]
    lat, lon = lax.axis_index("lat"), lax.axis_index("lon")
    lats, lons = lax.axis_size("lat"), lax.axis_size("lon")
    left, right = (lat, lax.rem(lon + lons - 1, lons)), (lat, lax.rem(lon + 1, lons))
    up, down = (lax.rem(lat + lats - 1, lats), lon), (lax.rem(lat + 1, lats), lon)
    barrier = pltpu.get_barrier_semaphore()
    for other in (left, right, up, down):
        pl.semaphore_signal(barrier, inc=1, device_id=other, device_id_type=MESH)
    seed = seed_ref[0, 0]
    row = 0
    for level, (rows, cols) in enumerate(shapes):
        e = ext[level]
        tall = max(rows, SUB)
        e[...] = jnp.zeros_like(e)
        e[SUB : SUB + rows, 0:cols] = latents[level][...] + hashed_noise(seed, level, (rows, cols))
        if cols >= LANES:
            send_l[row : row + tall, :] = e[SUB : SUB + tall, 0:LANES]
            send_r[row : row + tall, :] = e[SUB : SUB + tall, cols - LANES : cols]
        else:
            whole = e[SUB : SUB + tall, :]
            send_l[row : row + tall, :] = whole
            send_r[row : row + tall, :] = pltpu.roll(whole, LANES - cols, 1)
        row += tall
    pl.semaphore_wait(barrier, 4)

    def copy(src, dst, index, other):
        return pltpu.make_async_remote_copy(
            src_ref=src,
            dst_ref=dst,
            send_sem=ssem.at[index],
            recv_sem=rsem.at[index],
            device_id=other,
            device_id_type=MESH,
        )

    to_left = copy(send_l, recv_r, 0, left)
    to_right = copy(send_r, recv_l, 1, right)
    to_left.start()
    to_right.start()
    to_left.wait()
    to_right.wait()
    row = 0
    lane0 = 0
    for level, (rows, cols) in enumerate(shapes):
        e = ext[level]
        tall = max(rows, SUB)
        from_right = recv_r[row : row + tall, :]
        from_left = recv_l[row : row + tall, :]
        lane = iota((tall, LANES), 1)
        if cols >= LANES:
            e[SUB : SUB + tall, cols : cols + LANES] = jnp.where(
                lane < LANES // 2, from_right, from_left
            )
        else:
            whole = e[SUB : SUB + tall, :]
            moved = pltpu.roll(from_right, cols, 1)
            halo = jnp.where(
                lane < cols + 4, moved, jnp.where(lane >= LANES - 4, from_left, 0.0)
            )
            e[SUB : SUB + tall, :] = jnp.where(lane < cols, whole, halo)
        wide = width_of(cols)
        send_u[:, lane0 : lane0 + wide] = e[SUB : 2 * SUB, :]
        send_d[:, lane0 : lane0 + wide] = e[tall : tall + SUB, :]
        row += tall
        lane0 += wide
    to_up = copy(send_u, recv_b, 2, up)
    to_down = copy(send_d, recv_t, 3, down)
    to_up.start()
    to_down.start()
    to_up.wait()
    to_down.wait()
    keep_t = jnp.where(lat > 0, 1.0, 0.0).astype(F32)
    keep_b = jnp.where(lat < lats - 1, 1.0, 0.0).astype(F32)
    lane0 = 0
    for level, (rows, cols) in enumerate(shapes):
        e = ext[level]
        wide = width_of(cols)
        top = recv_t[:, lane0 : lane0 + wide] * keep_t
        bottom = recv_b[:, lane0 : lane0 + wide] * keep_b
        reach = min(rows, SUB)
        e[SUB - reach : SUB, :] = top[:reach]
        e[SUB + rows : SUB + rows + reach, :] = bottom[:reach]
        lane0 += wide


def sum_kernel(part, total, row, col, send_sem, recv_sem):
    place = {"lon": lax.axis_index("lon"), "lat": lax.axis_index("lat")}
    barrier = pltpu.get_barrier_semaphore()

    def peers(axis):
        size = lax.axis_size(axis)
        for d in range(1, size):
            yield d - 1, {**place, axis: lax.rem(place[axis] + d, size)}

    count = 0
    for axis in ("lon", "lat"):
        for _, other in peers(axis):
            pl.semaphore_signal(
                barrier, inc=1, device_id=(other["lat"], other["lon"]), device_id_type=MESH
            )
            count += 1
    row[place["lon"]] = part[...]
    pl.semaphore_wait(barrier, count)
    first = 0
    for axis, slots in (("lon", row), ("lat", col)):
        mine = slots.at[place[axis]]
        copies = [
            pltpu.make_async_remote_copy(
                src_ref=mine,
                dst_ref=mine,
                send_sem=send_sem.at[first + d],
                recv_sem=recv_sem.at[first + d],
                device_id=(other["lat"], other["lon"]),
                device_id_type=MESH,
            )
            for d, other in peers(axis)
        ]
        for copy in copies:
            copy.start()
        for copy in copies:
            copy.wait()
        first += len(copies)
        added = slots[0]
        for d in range(1, lax.axis_size(axis)):
            added = added + slots[d]
        if axis == "lon":
            col[place["lat"]] = added
        else:
            total[...] = added


def dot(a, b):
    return jnp.dot(a, b, preferred_element_type=F32)


def parts(x, count):
    out = []
    for _ in range(count):
        piece = x.astype(BF)
        out.append(piece)
        x = x - piece.astype(F32)
    return out


def dot_first(a, b):
    return lax.dot_general(a, b, (((0,), (0,)), ((), ())), preferred_element_type=F32)


def dot_pairs(a, x):
    hi, lo = parts(x, 2)
    m, k = a.shape[0] // 2, a.shape[1]
    if k == 2 * x.shape[0]:
        p = dot(a, jnp.concatenate([hi, lo], 0))
        return p[:m] + p[m:]
    p = dot(a, hi)
    return p[:m] + (p[m:] + dot(a[:m], lo))


def div_24(x):
    return (x * 2731) >> 16


def looped(count, most, body, carry):
    each = next(k for k in range(min(most, count), 0, -1) if count % k == 0)

    def turn(t, carry):
        for k in range(each):
            carry = body(t * each + k, carry)
        return carry

    if each == count:
        return turn(0, carry)
    return lax.fori_loop(0, count // each, turn, carry)


def aligned(value, by):
    return value if isinstance(value, int) else pl.multiple_of(value, by)


def one_hot(flag):
    return jnp.where(flag, 1.0, 0.0).astype(BF)


def laplace_bits(offset, spread):
    magnitude = jnp.abs(offset)
    t = 1.0 / spread
    series = t * (1.0 - t * (0.5 - t * (1.0 / 6 - t * (1.0 / 24 - t * (1.0 / 120)))))
    gap = jnp.where(t < 0.1, series, 1.0 - jnp.exp(-t))
    outer = -log_two - (jnp.maximum(magnitude, 0.5) - 0.5) / spread + jnp.log(gap)
    inner_offset = jnp.clip(offset, -0.5, 0.5)
    inner = jnp.log(
        1.0
        - 0.5 * (jnp.exp(-(0.5 - inner_offset) / spread) + jnp.exp(-(0.5 + inner_offset) / spread))
    )
    return jnp.where(magnitude >= 0.5, outer, inner) * (-1.0 / log_two)


def local_kernel(shapes, ch, bands, pixel_count, *refs):
    n = len(shapes)
    ext = refs[:n]
    (
        target, parity, anchor, mix_l, mix_h, w_first, w_second, w_output, c_in, c_mid, c_out,
        recon, bits_out, part, ups, second, third, fourth,
    ) = refs[n:]
    lat, lon = lax.axis_index("lat"), lax.axis_index("lon")
    lats = lax.axis_size("lat")
    rows_dev, cols_dev = shapes[0]
    wide = width_of(cols_dev)
    deep = SUB * ch
    reach = (SUB + 2) * ch

    lane_ch = iota((ch, deep), 1)
    fold = one_hot(lane_ch - ch * div_24(lane_ch) == iota((ch, deep), 0))
    same_row = div_24(iota((deep, deep), 0)) == div_24(iota((deep, deep), 1))

    def block_diagonal(w):
        return jnp.where(same_row, jnp.concatenate([dot(w, fold)] * SUB, 0), 0.0).astype(BF)

    def row_inside(w):
        k = w.shape[0]
        spread = one_hot((iota((k, k * SUB), 1) >> 3) == iota((k, k * SUB), 0))
        shape = (deep, k * SUB)
        keep = (iota(shape, 1) & 7) == div_24(iota(shape, 0))
        return jnp.where(keep, jnp.concatenate([dot_first(w, spread)] * SUB, 0), 0.0).astype(BF)

    def rows_out(w):
        wide_w = dot(w, fold)
        grown = jnp.concatenate(
            [jnp.broadcast_to(wide_w[o : o + 1], (SUB, deep)) for o in range(w.shape[0])], 0
        )
        shape = (w.shape[0] * SUB, deep)
        keep = (iota(shape, 0) & 7) == div_24(iota(shape, 1))
        return jnp.where(keep, grown, 0.0).astype(BF)

    t_levels = row_inside(mix_l[...])
    t_hidden = block_diagonal(mix_h[...])
    a_in = jnp.concatenate([row_inside(p) for p in parts(c_in[...], 2)], 0)
    a_in = jnp.concatenate([a_in, a_in], 1)
    a_mid = jnp.concatenate([block_diagonal(p) for p in parts(c_mid[...], 2)], 0)
    a_out = jnp.concatenate([rows_out(p) for p in parts(c_out[...], 2)], 0)

    lane_re = iota((ch, reach), 1)
    fold_re = one_hot(lane_re - ch * div_24(lane_re) == iota((ch, reach), 0))
    step = div_24(iota((deep, reach), 1)) - div_24(iota((deep, reach), 0))
    step_out = div_24(iota((bands * SUB, reach), 1)) - (iota((bands * SUB, reach), 0) & 7)

    def conv_taps(w):
        grown = [[dot(w[a, b], fold_re) for b in range(3)] for a in range(3)]
        out = []
        for b in range(3):
            total = jnp.zeros((deep, reach), F32)
            for a in range(3):
                total = jnp.where(step == a, jnp.concatenate([grown[a][b]] * SUB, 0), total)
            out.append(total.astype(BF))
        return jnp.concatenate(out, 0)

    def output_taps():
        grown_out = [[dot(w_output[o, a], fold_re) for a in range(3)] for o in range(bands)]
        out = []
        for b in range(3):
            total = jnp.zeros((bands * SUB, reach), F32)
            for a in range(3):
                grown = jnp.concatenate(
                    [
                        jnp.broadcast_to(grown_out[o][a][b : b + 1], (SUB, reach))
                        for o in range(bands)
                    ],
                    0,
                )
                total = jnp.where(step_out == a, grown, total)
            out.append(total)
        return jnp.concatenate(out, 0).astype(BF)

    t_first = conv_taps(w_first)
    t_second = conv_taps(w_second)
    t_output = output_taps()

    tall_up = ups.shape[1]
    ups[0] = ext[0][SUB - 3 : SUB - 3 + tall_up, :]
    for level in range(1, n):
        rows, cols = shapes[level]
        e = ext[level]
        scale = 2.0 ** -level
        shape = (tall_up, e.shape[0])
        where_to = ((iota(shape, 0) - 3).astype(F32) + 0.5) * scale - 0.5
        along = jnp.maximum(
            0.0, 1.0 - jnp.abs(where_to - (iota(shape, 1) - SUB).astype(F32))
        ).astype(BF)
        hi, mid, lo = [dot(along, p) for p in parts(e[...], 3)]
        grown = hi + (mid + lo)
        shape = (e.shape[1], wide)
        pixel = iota(shape, 1)
        pixel = jnp.where(pixel < cols_dev + LANES // 2, pixel, pixel - wide)
        cell = iota(shape, 0)
        cell = jnp.where(cell < (cols + e.shape[1]) // 2, cell, cell - e.shape[1])
        where_to = (pixel.astype(F32) + 0.5) * scale - 0.5
        along = jnp.maximum(0.0, 1.0 - jnp.abs(where_to - cell.astype(F32))).astype(BF)
        hi, mid, lo = [dot(p, along) for p in parts(grown, 3)]
        ups[level] = hi + (mid + lo)

    def inside(field, start, margin):
        index = iota(field.shape, 0)
        begin = margin - start - lat * rows_dev
        keep = (index >= begin * ch) & (index < (begin + rows_dev * lats) * ch)
        return jnp.where(keep, field, 0.0)

    def mix_step(g, carry):
        here = pl.ds(aligned(g * SUB, SUB), SUB)
        x = jnp.concatenate([ups[level, here, :] for level in range(n)], 0).astype(BF)
        f = jnp.maximum(dot(t_levels, x), 0.0).astype(BF)
        s = jnp.maximum(dot(t_hidden, f), 0.0)
        second[pl.ds(aligned(g * deep, deep), deep), :] = inside(s, g * SUB, 3).astype(BF)
        return carry

    looped(tall_up // SUB, 3, mix_step, 0)

    def conv_pass(src, dst, weights, count, margin):
        def step_fn(k, carry):
            start = min(k * SUB, count - SUB) if isinstance(k, int) else jnp.minimum(k * SUB, count - SUB)
            at = aligned(start * ch, 2 * ch)
            x = src[pl.ds(at, reach), :]
            p = dot(weights, x)
            c = (
                p[deep : 2 * deep]
                + pltpu.roll(p[:deep], 1, 1)
                + pltpu.roll(p[2 * deep :], wide - 1, 1)
            )
            r = x.astype(F32)[ch : ch + deep] + jnp.maximum(c, 0.0)
            dst[pl.ds(at, deep), :] = inside(r, start, margin).astype(BF)
            return carry

        looped((count + SUB - 1) // SUB, 3, step_fn, 0)

    conv_pass(second, third, t_first, rows_dev + 4, 2)
    conv_pass(third, fourth, t_second, rows_dev + 2, 1)

    def output_step(k, carry):
        squares, grad = carry
        x = fourth[pl.ds(aligned(k * deep, deep), reach), :]
        p = dot(t_output, x)
        m = bands * SUB
        c = p[m : 2 * m] + pltpu.roll(p[:m], 1, 1) + pltpu.roll(p[2 * m :], wide - 1, 1)
        c = c[:, :cols_dev]
        here = pl.ds(aligned(k * SUB, SUB), SUB)
        for o in range(bands):
            recon[o, here, :] = c[o * SUB : (o + 1) * SUB]
        error = c - jnp.concatenate([target[o, here, :] for o in range(bands)], 0)
        slope = (2.0 * error / pixel_count).astype(BF).astype(F32)
        slope = jnp.concatenate([slope, jnp.zeros((m, wide - cols_dev), F32)], 1)
        slopes = jnp.concatenate(
            [pltpu.roll(slope, wide - 1, 1), slope, pltpu.roll(slope, 1, 1)], 0
        ).astype(BF)
        grad = grad + lax.dot_general(
            slopes, x, (((1,), (1,)), ((), ())), preferred_element_type=F32
        )
        return squares + error * error, grad

    m = bands * SUB
    totals = []
    m = bands * SUB
    for level, (rows, cols) in enumerate(shapes):
        e = ext[level]
        cover = max(cols, LANES)
        full = e.shape[1]
        scale = anchor[level]
        odd = lat * rows + lon * cols + parity[level]

        blocks = 2 if rows % (2 * SUB) == 0 else 1

        def rate_step(g, total, blocks=blocks, level=level, rows=rows, cols=cols, e=e, cover=cover, full=full, scale=scale, odd=odd):
            def context_of(block):
                window = e[pl.ds(aligned(block * SUB, SUB), 3 * SUB), :]
                moved = {i: window[SUB + i : 2 * SUB + i] for i in range(-2, 3)}
                near = [
                    (moved[i] if j == 0 else pltpu.roll(moved[i], (-j) % full, 1))[:, :cover]
                    for i, j in context_steps
                ]
                return near, moved[0][:, :cover]

            row, col = iota((SUB, cover), 0), iota((SUB, cover), 1)
            first = ((row + col + odd) & 1) == 0
            near, here = context_of(g * blocks)
            cells = [here]
            if blocks == 2:
                later, here = context_of(g * blocks + 1)
                cells.append(here)
                near = [
                    jnp.where(first, pltpu.roll(q, cover - 1, 1), p) for p, q in zip(near, later)
                ]
            inner = jnp.maximum(dot_pairs(a_in, jnp.concatenate(near, 0)), 0.0)
            outer = jnp.maximum(dot_pairs(a_mid, inner), 0.0)
            raw = dot_pairs(a_out, outer)
            mu, sigma = raw[:SUB], raw[SUB:]
            soft = 0.1 + jnp.maximum(sigma, 0.0) + jnp.log1p(jnp.exp(-jnp.abs(sigma)))
            for k, here in enumerate(cells):
                if k == 1:
                    mu, soft = pltpu.roll(mu, 1, 1), pltpu.roll(soft, 1, 1)
                centre = jnp.where(first, 0.0, mu)
                spread = jnp.where(first, scale, soft)
                bits = laplace_bits(here - centre, spread)
                if level == 0:
                    bits_out[pl.ds(aligned((g * blocks + k) * SUB, SUB), SUB), :] = bits
                if rows < SUB or cols < LANES:
                    bits = jnp.where((row < rows) & (col < cols), bits, 0.0)
                total = total + bits
            return total

        count = max(1, rows // (SUB * blocks))
        start = jnp.zeros((SUB, cover), F32)
        if level == 0:

            def both_steps(g, carry):
                out, total = carry
                for k in range(blocks):
                    out = output_step(g * blocks + k, out)
                return out, rate_step(g, total)

            start_out = (jnp.zeros((m, cols_dev), F32), jnp.zeros((3 * m, reach), F32))
            (squares, grad), total = looped(count, 2, both_steps, (start_out, start))
        else:
            total = looped(count, 2, rate_step, start)
        totals.append(jnp.sum(total) * (1.0 / (rows * cols * lats * lax.axis_size("lon"))))
    pad = -reach % LANES
    grad = jnp.concatenate([grad, jnp.zeros((3 * m, pad), F32)], 1)
    line = iota(grad.shape, 0) & 7
    moved = grad
    for y in range(1, SUB):
        moved = jnp.where(line == y, pltpu.roll(grad, reach + pad - y * ch, 1), moved)
    folded = jnp.sum(moved[:, :LANES].reshape(3 * bands, SUB, LANES), axis=1)
    sums = jnp.concatenate([folded, jnp.zeros((part.shape[0] - 3 * bands, LANES), F32)], 0)

    shape = part.shape
    last = iota(shape, 0) == 3 * bands

    def put(sums, lane, value):
        return jnp.where(last & (iota(shape, 1) == lane), value, sums)

    sums = put(sums, 0, jnp.sum(squares) * (1.0 / pixel_count))

    for level, value in enumerate(totals):
        sums = put(sums, 1 + level, value)
    part[...] = sums


def local(target, *args):
    latents = args[:-11]
    (
        tile_seeds, anchor_parity, anchor_scale, mix_levels, mix_hidden,
        conv_first, conv_second, conv_output, context_in, context_mid, context_out,
    ) = args[-11:]
    n = len(latents)
    shapes = [x.shape for x in latents]
    bands, rows_dev, cols_dev = target.shape
    ch = mix_hidden.shape[0]
    devices = lax.axis_size("lat") * lax.axis_size("lon")
    pixel_count = float(bands * rows_dev * cols_dev * devices)
    vmem = pl.BlockSpec(memory_space=pltpu.VMEM)
    smem = pl.BlockSpec(memory_space=pltpu.SMEM)
    wides = [width_of(c) for _, c in shapes]
    talls = [max(r, SUB) for r, _ in shapes]
    edge = pltpu.VMEM((sum(talls), LANES), F32)
    belt = pltpu.VMEM((SUB, sum(wides)), F32)
    extended = pl.pallas_call(
        functools.partial(halo_kernel, shapes),
        out_shape=[
            jax.ShapeDtypeStruct((t + 2 * SUB, w), F32) for t, w in zip(talls, wides)
        ],
        in_specs=[smem] + [vmem] * n,
        out_specs=[vmem] * n,
        scratch_shapes=[edge] * 4
        + [belt] * 4
        + [pltpu.SemaphoreType.DMA((4,)), pltpu.SemaphoreType.DMA((4,))],
        compiler_params=pltpu.CompilerParams(
            collective_id=0, has_side_effects=True, vmem_limit_bytes=16 * 2**20
        ),
        name="halo",
    )(tile_seeds, *latents)
    convs = [w.transpose(2, 3, 0, 1) for w in (conv_first, conv_second)]
    convs.append(conv_output.transpose(0, 2, 3, 1))
    wide = wides[0]
    tall_up = rows_dev + SUB
    recon, bits, part = pl.pallas_call(
        functools.partial(local_kernel, shapes, ch, bands, pixel_count),
        out_shape=[
            jax.ShapeDtypeStruct(target.shape, F32),
            jax.ShapeDtypeStruct((rows_dev, cols_dev), F32),
            jax.ShapeDtypeStruct((2 * SUB, LANES), F32),
        ],
        in_specs=[vmem] * (n + 1) + [smem] * 2 + [vmem] * 8,
        out_specs=[vmem] * 3,
        scratch_shapes=[
            pltpu.VMEM((n, tall_up, wide), F32),
            pltpu.VMEM((tall_up * ch, wide), BF),
            pltpu.VMEM(((rows_dev + 4) * ch, wide), BF),
            pltpu.VMEM(((rows_dev + 2) * ch, wide), BF),
        ],
        compiler_params=pltpu.CompilerParams(vmem_limit_bytes=48 * 2**20),
        name="step",
    )(
        *extended, target, anchor_parity, anchor_scale, mix_levels.T, mix_hidden,
        *convs, context_in.T, context_mid, context_out,
    )
    lats, lons = lax.axis_size("lat"), lax.axis_size("lon")
    total = pl.pallas_call(
        sum_kernel,
        out_shape=jax.ShapeDtypeStruct(part.shape, F32),
        in_specs=[vmem],
        out_specs=vmem,
        scratch_shapes=[
            pltpu.VMEM((lons,) + part.shape, F32),
            pltpu.VMEM((lats,) + part.shape, F32),
            pltpu.SemaphoreType.DMA((lats + lons - 2,)),
            pltpu.SemaphoreType.DMA((lats + lons - 2,)),
        ],
        compiler_params=pltpu.CompilerParams(
            collective_id=1, has_side_effects=True, vmem_limit_bytes=8 * 2**20
        ),
        name="sums",
    )(part)
    grad = total[: 3 * bands, : 3 * ch].reshape(3, bands, 3, ch).transpose(1, 3, 2, 0)
    loss_terms = total[3 * bands, : n + 1]
    return (recon, bits, loss_terms, grad)


def solution(mesh):
    both = P("lat", "lon")
    return jax.shard_map(
        local,
        mesh=mesh,
        in_specs=(P(None, "lat", "lon"),) + (both,) * 7 + (P(),) * 10,
        out_specs=(P(None, "lat", "lon"), both, P(), P()),
        check_vma=False,
    )
```
